1024 devices in a mesh: seq: 16 (over x, z_lo), inner: 64 (over y, z_hi, core).
Axes of the slice: x: 8, y: 8, z: 8 (z_hi: 4, z_lo: 2; z = z_hi * 2 + z_lo), core: 2. Of those that a mesh axis runs over, the one named last changes fastest.
Arguments:
- queries: bfloat16 [16384, 8192], P('seq', 'inner'), may hold values from -6 to 6
- key_vectors: bfloat16 [16384, 8192], P('seq', 'inner'), may hold values from -6 to 6
- value_vectors: bfloat16 [16384, 8192], P('seq', 'inner'), may hold values from -6 to 6
- out_grad: bfloat16 [16384, 8192], P('seq', 'inner'), may hold values from -6 to 6
Outputs:
- attended: bfloat16 [16384, 8192], P('seq', 'inner')
- query_grad: bfloat16 [16384, 8192], P('seq', 'inner')
- key_grad: bfloat16 [16384, 8192], P('seq', 'inner')
- value_grad: bfloat16 [16384, 8192], P('seq', 'inner')
The draws below stay inside these ranges and needn't reach their ends.
All inputs are finite; a program needn't handle non-finite values.
Results may differ from the reference program's by a relative error of at most 0.0058.
Values sent between devices are 32-bit elements; how exact they have to be, the bound alone decides.
No kernel may reach another device: no remote copies, remote signals or barrier semaphores. Data moves between devices by JAX's collectives and lax.ppermute only.
A program may use at most 32 MiB of HBM per device.

```python
import jax
import jax.numpy as jnp
from jax import lax

DK = 128
HEADS = 32
HALF = 1024
BLOCK = 512
TOKENS = 32768
COLS = 4096
N_SEQ = 16


def shard_levels(own_key, extent, cuts, smallest, high):
    def one(dim, blocks):
        steps = jax.random.uniform(jax.random.fold_in(jax.random.fold_in(own_key, 6), dim), (blocks,), jnp.float32, smallest / len(cuts), high / len(cuts))
        return jnp.repeat(jnp.exp(steps), extent[dim] // blocks).reshape((-1,) + (1,) * (len(extent) - dim - 1))

    factor_of = one(*cuts[0])
    for cut in cuts[1:]:
        factor_of = factor_of * one(*cut)
    return factor_of


def noise(own_key, shape, deviation, most, cuts=(), kind=jnp.bfloat16):
    factor_of = shard_levels(own_key, shape, cuts, -0.22, 0.18) if cuts else 1.0
    drawn = jax.random.normal(own_key, shape, jnp.float32) * deviation * factor_of
    return jnp.minimum(jnp.maximum(drawn, -most), most).astype(kind)


def setup_inputs(seed: int = 0) -> dict:
    seeds = jax.random.split(jax.random.key(seed), 5)
    return {
        "queries": noise(seeds[0], (TOKENS // 2, 2 * COLS), 1.0, 6.0, ((0, 16), (1, 64))),
        "key_vectors": noise(seeds[1], (TOKENS // 2, 2 * COLS), 1.0, 6.0, ((0, 16), (1, 64))),
        "value_vectors": noise(seeds[2], (TOKENS // 2, 2 * COLS), 1.0, 6.0, ((0, 16), (1, 64))),
        "out_grad": noise(seeds[3], (TOKENS // 2, 2 * COLS), 1.0, 6.0, ((0, 16), (1, 64))),
    }


def from_layout(array):
    shaped = array.reshape(N_SEQ, HALF, HEADS, 2, DK)
    shaped = jnp.transpose(shaped, (0, 3, 1, 2, 4))
    return shaped.reshape(TOKENS, HEADS * DK)

def to_layout(array):
    shaped = array.reshape(N_SEQ, 2, HALF, HEADS, DK)
    shaped = jnp.transpose(shaped, (0, 2, 3, 1, 4))
    return shaped.reshape(TOKENS // 2, 2 * HEADS * DK)

def heads_blocks(array):
    shaped = from_layout(array).reshape(TOKENS // BLOCK, BLOCK, HEADS, DK)
    return jnp.transpose(shaped, (0, 2, 1, 3))

def unblock(array):
    return to_layout(jnp.transpose(array, (0, 2, 1, 3)).reshape(TOKENS, HEADS * DK))

def rounded(values_f):
    return lax.optimization_barrier(values_f.astype(jnp.bfloat16)).astype(jnp.float32)

def prepare(block_index, query_b, key_b, value_b, grad_b):
    row_ids = jnp.arange(BLOCK, dtype=jnp.int32)
    causal = row_ids[:, None] >= row_ids[None, :]
    position = (block_index * BLOCK + row_ids).astype(jnp.float32)
    scaling = 1.0 / jnp.sqrt(DK * (position + 1.0))
    query_f = query_b.astype(jnp.float32)
    key_f = key_b.astype(jnp.float32)
    value_f = value_b.astype(jnp.float32)
    scaled_grad = rounded(scaling[None, :, None] * grad_b.astype(jnp.float32))
    scores = jnp.einsum('hbd,hcd->hbc', query_f, key_f)
    weights = rounded(jnp.where(causal[None], scores, 0.0))
    grad_scores = rounded(jnp.where(causal[None], jnp.einsum('hbv,hcv->hbc', scaled_grad, value_f), 0.0))
    return (scaling, query_f, key_f, value_f, scaled_grad, weights, grad_scores)

def reference(queries, key_vectors, value_vectors, out_grad):
    block_ids = jnp.arange(TOKENS // BLOCK, dtype=jnp.int32)
    inputs = (block_ids, heads_blocks(queries), heads_blocks(key_vectors), heads_blocks(value_vectors), heads_blocks(out_grad))
    zero_state = jnp.zeros((HEADS, DK, DK), jnp.float32)

    def forward(kv_state, pieces):
        scaling, query_f, key_f, value_f, scaled_grad, weights, grad_scores = prepare(*pieces)
        kv_used = rounded(kv_state)
        local = jnp.einsum('hbc,hcv->hbv', weights, value_f)
        carried = jnp.einsum('hbd,hdv->hbv', query_f, kv_used)
        attended = ((local + carried) * scaling[None, :, None]).astype(jnp.bfloat16)
        query_local = jnp.einsum('hbc,hcd->hbd', grad_scores, key_f)
        query_carried = jnp.einsum('hbv,hdv->hbd', scaled_grad, kv_used)
        query_grad = (query_local + query_carried).astype(jnp.bfloat16)
        kv_state = kv_state + jnp.einsum('hcd,hcv->hdv', key_f, value_f)
        return (kv_state, (attended, query_grad))

    def backward(back_state, pieces):
        scaling, query_f, key_f, value_f, scaled_grad, weights, grad_scores = prepare(*pieces)
        back_used = rounded(back_state)
        key_local = jnp.einsum('hbc,hbd->hcd', grad_scores, query_f)
        key_carried = jnp.einsum('hcv,hdv->hcd', value_f, back_used)
        key_grad = (key_local + key_carried).astype(jnp.bfloat16)
        value_local = jnp.einsum('hbc,hbv->hcv', weights, scaled_grad)
        value_carried = jnp.einsum('hcd,hdv->hcv', key_f, back_used)
        value_grad = (value_local + value_carried).astype(jnp.bfloat16)
        back_state = back_state + jnp.einsum('hbd,hbv->hdv', query_f, scaled_grad)
        return (back_state, (key_grad, value_grad))
    final_state, forward_out = lax.scan(forward, zero_state, inputs)
    final_back, backward_out = lax.scan(backward, zero_state, inputs, reverse=True)
    return (unblock(forward_out[0]), unblock(forward_out[1]), unblock(backward_out[0]), unblock(backward_out[1]))
```

```python
import functools

import jax
import jax.numpy as jnp
from jax import lax
from jax.experimental import pallas as pl
from jax.experimental.pallas import tpu as pltpu
from jax.sharding import PartitionSpec as P

BLOCK = 512
SUB = 256
AXES = ("seq", "inner")
F32 = jnp.float32
BF16 = jnp.bfloat16


def dot(a, b, ca, cb):
    return lax.dot_general(a, b, (((ca,), (cb,)), ((), ())), preferred_element_type=F32)


def scaling_of(start, rows, width):
    row = lax.broadcasted_iota(jnp.int32, (rows, width), 0)
    position = (start + row).astype(F32)
    return 1.0 / jnp.sqrt(width * (position + 1.0))


def first_position(half_rows):
    return (lax.axis_index("seq") * 2 + lax.axis_index("inner") % 2) * half_rows


def outer_kernel(q_ref, k_ref, v_ref, o_ref, send_ref, keep_ref, grad_ref):
    half_rows, width = q_ref.shape
    start = first_position(half_rows)
    kv, back = [], []
    for b in range(half_rows // BLOCK):
        rows = pl.ds(b * BLOCK, BLOCK)
        scaling = scaling_of(start + b * BLOCK, BLOCK, width)
        grad = (scaling * o_ref[rows, :].astype(F32)).astype(BF16)
        grad_ref[rows, :] = grad
        kv.append(dot(k_ref[rows, :], v_ref[rows, :], 0, 0))
        back.append(dot(q_ref[rows, :], grad, 0, 0))
    keep_ref[:width, :] = kv[0]
    keep_ref[width:, :] = back[1]
    send_ref[:width, :] = kv[0] + kv[1]
    send_ref[width:, :] = back[0] + back[1]


def scan_kernel(parts_ref, out_ref):
    count = parts_ref.shape[0]
    me = lax.axis_index("seq") * 2 + lax.axis_index("inner") % 2
    is_kv = me < count // 2
    zero = jnp.zeros(parts_ref.shape[1:], F32)
    before = [zero]
    for i in range(count - 1):
        before.append(before[-1] + parts_ref[i])
    after = zero
    for i in reversed(range(count)):
        out_ref[i] = jnp.where(is_kv, before[i], after)
        after = after + parts_ref[i]


def main_kernel(q_ref, k_ref, v_ref, g_ref, state_ref, keep_ref, att_ref, qg_ref, kg_ref, vg_ref):
    half_rows, width = q_ref.shape
    start = first_position(half_rows)
    row = lax.broadcasted_iota(jnp.int32, (SUB, SUB), 0)
    col = lax.broadcasted_iota(jnp.int32, (SUB, SUB), 1)
    causal = row >= col
    kv0 = state_ref[:width, :]
    back1 = state_ref[width:, :]
    kv_used = [kv0.astype(BF16), (kv0 + keep_ref[:width, :]).astype(BF16)]
    back_used = [(back1 + keep_ref[width:, :]).astype(BF16), back1.astype(BF16)]
    for b in range(half_rows // BLOCK):
        tiles = [pl.ds(b * BLOCK + i * SUB, SUB) for i in range(BLOCK // SUB)]
        n = len(tiles)
        q = [q_ref[t, :] for t in tiles]
        k = [k_ref[t, :] for t in tiles]
        v = [v_ref[t, :] for t in tiles]
        g = [g_ref[t, :] for t in tiles]
        att = [dot(q[i], kv_used[b], 1, 0) for i in range(n)]
        qg = [dot(g[i], kv_used[b], 1, 1) for i in range(n)]
        kg = [dot(v[i], back_used[b], 1, 1) for i in range(n)]
        vg = [dot(k[i], back_used[b], 1, 0) for i in range(n)]
        for i in range(n):
            for j in range(i + 1):
                w = dot(q[i], k[j], 1, 1)
                s = dot(g[i], v[j], 1, 1)
                if i == j:
                    w = jnp.where(causal, w, 0.0)
                    s = jnp.where(causal, s, 0.0)
                w = w.astype(BF16)
                s = s.astype(BF16)
                att[i] = att[i] + dot(w, v[j], 1, 0)
                qg[i] = qg[i] + dot(s, k[j], 1, 0)
                kg[j] = kg[j] + dot(s, q[i], 0, 0)
                vg[j] = vg[j] + dot(w, g[i], 0, 0)
        for i in range(n):
            scaling = scaling_of(start + b * BLOCK + i * SUB, SUB, width)
            att_ref[tiles[i], :] = (att[i] * scaling).astype(BF16)
            qg_ref[tiles[i], :] = qg[i].astype(BF16)
            kg_ref[tiles[i], :] = kg[i].astype(BF16)
            vg_ref[tiles[i], :] = vg[i].astype(BF16)


def call(kernel, outs, limit):
    return pl.pallas_call(
        kernel,
        out_shape=outs,
        compiler_params=pltpu.CompilerParams(vmem_limit_bytes=limit),
    )


def per_device(groups, queries, key_vectors, value_vectors, out_grad):
    half_rows, width = queries.shape
    rows16 = jax.ShapeDtypeStruct((half_rows, width), BF16)
    states = jax.ShapeDtypeStruct((2 * width, width), F32)
    send, keep, grad = call(outer_kernel, (states, states, rows16), 2**24)(
        queries, key_vectors, value_vectors, out_grad
    )
    count = len(groups[0])
    parts = send.reshape(count, 2 * width // count, width)
    parts = lax.all_to_all(parts, AXES, 0, 0, axis_index_groups=groups)
    parts = call(scan_kernel, jax.ShapeDtypeStruct(parts.shape, F32), 2**23)(parts)
    parts = lax.all_to_all(parts, AXES, 0, 0, axis_index_groups=groups)
    state = parts.reshape(2 * width, width)
    return call(main_kernel, (rows16,) * 4, 2**24)(
        queries, key_vectors, value_vectors, grad, state, keep
    )


def solution(mesh):
    n_seq, n_inner = mesh.shape["seq"], mesh.shape["inner"]
    groups = [
        [s * n_inner + 2 * h + side for s in range(n_seq) for side in range(2)]
        for h in range(n_inner // 2)
    ]
    spec = P("seq", "inner")
    return jax.shard_map(
        functools.partial(per_device, groups),
        mesh=mesh,
        in_specs=(spec,) * 4,
        out_specs=(spec,) * 4,
        check_vma=False,
    )
```

```python
import functools

import jax
import jax.numpy as jnp
from jax import lax
from jax.experimental import pallas as pl
from jax.experimental.pallas import tpu as pltpu
from jax.sharding import PartitionSpec as P

BLOCK = 512
SUB = 256
AXES = ("seq", "inner")
F32 = jnp.float32
BF16 = jnp.bfloat16


def dot(a, b, ca, cb):
    return lax.dot_general(a, b, (((ca,), (cb,)), ((), ())), preferred_element_type=F32)


def scaling_of(start, rows, width):
    row = lax.broadcasted_iota(jnp.int32, (rows, width), 0)
    position = (start + row).astype(F32)
    return 1.0 / jnp.sqrt(width * (position + 1.0))


def first_position(half_rows):
    return (lax.axis_index("seq") * 2 + lax.axis_index("inner") % 2) * half_rows


def outer_kernel(
    q_hbm, k_hbm, v_hbm, o_hbm, send_ref, keep_ref, q_ref, k_ref, v_ref, grad_ref, o_ref, sems
):
    half_rows, width = q_ref.shape
    start = first_position(half_rows)
    pairs = ((k_hbm, k_ref), (v_hbm, v_ref), (o_hbm, o_ref), (q_hbm, q_ref))
    copies = []
    for b in range(half_rows // BLOCK):
        rows = pl.ds(b * BLOCK, BLOCK)
        for i, (source, target) in enumerate(pairs):
            copies.append(
                pltpu.make_async_copy(source.at[rows, :], target.at[rows, :], sems.at[b, i])
            )
    for copy in copies:
        copy.start()
    kv, back = [], []
    for b in range(half_rows // BLOCK):
        rows = pl.ds(b * BLOCK, BLOCK)
        scaling = scaling_of(start + b * BLOCK, BLOCK, width)
        copies[4 * b].wait()
        copies[4 * b + 1].wait()
        kv.append(dot(k_ref[rows, :], v_ref[rows, :], 0, 0))
        copies[4 * b + 2].wait()
        grad = (scaling * o_ref[rows, :].astype(F32)).astype(BF16)
        grad_ref[rows, :] = grad
        copies[4 * b + 3].wait()
        back.append(dot(q_ref[rows, :], grad, 0, 0))
    keep_ref[:width, :] = kv[0]
    keep_ref[width:, :] = back[1]
    send_ref[:width, :] = kv[0] + kv[1]
    send_ref[width:, :] = back[0] + back[1]


def scan_kernel(parts_ref, out_ref):
    count = parts_ref.shape[0]
    me = lax.axis_index("seq") * 2 + lax.axis_index("inner") % 2
    is_kv = me < count // 2
    zero = jnp.zeros(parts_ref.shape[1:], F32)
    before = [zero]
    for i in range(count - 1):
        before.append(before[-1] + parts_ref[i])
    after = zero
    for i in reversed(range(count)):
        out_ref[i] = jnp.where(is_kv, before[i], after)
        after = after + parts_ref[i]


def local_kernel(q_ref, k_ref, v_ref, g_ref, att_ref, qg_ref, kg_ref, vg_ref):
    half_rows, width = q_ref.shape
    row = lax.broadcasted_iota(jnp.int32, (SUB, SUB), 0)
    col = lax.broadcasted_iota(jnp.int32, (SUB, SUB), 1)
    causal = row >= col
    for b in range(half_rows // BLOCK):
        tiles = [pl.ds(b * BLOCK + i * SUB, SUB) for i in range(BLOCK // SUB)]
        n = len(tiles)
        q = [q_ref[t, :] for t in tiles]
        k = [k_ref[t, :] for t in tiles]
        v = [v_ref[t, :] for t in tiles]
        g = [g_ref[t, :] for t in tiles]
        att, qg, kg, vg = ([0.0] * n for _ in range(4))
        for i in range(n):
            for j in range(i + 1):
                w = dot(q[i], k[j], 1, 1)
                s = dot(g[i], v[j], 1, 1)
                if i == j:
                    w = jnp.where(causal, w, 0.0)
                    s = jnp.where(causal, s, 0.0)
                w = w.astype(BF16)
                s = s.astype(BF16)
                att[i] = att[i] + dot(w, v[j], 1, 0)
                qg[i] = qg[i] + dot(s, k[j], 1, 0)
                kg[j] = kg[j] + dot(s, q[i], 0, 0)
                vg[j] = vg[j] + dot(w, g[i], 0, 0)
        for i in range(n):
            att_ref[tiles[i], :] = att[i]
            qg_ref[tiles[i], :] = qg[i]
            kg_ref[tiles[i], :] = kg[i]
            vg_ref[tiles[i], :] = vg[i]


def final_kernel(
    q_ref, k_ref, v_ref, g_ref, state_ref, keep_ref,
    att_in, qg_in, kg_in, vg_in,
    att_hbm, qg_hbm, kg_hbm, vg_hbm,
    att_ref, qg_ref, kg_ref, vg_ref, sems,
):
    half_rows, width = q_ref.shape
    start = first_position(half_rows)
    kv0 = state_ref[:width, :]
    back1 = state_ref[width:, :]
    kv_used = [kv0.astype(BF16), (kv0 + keep_ref[:width, :]).astype(BF16)]
    back_used = [(back1 + keep_ref[width:, :]).astype(BF16), back1.astype(BF16)]
    copies = []

    def put(value, buffer, out, rows):
        buffer[rows, :] = value.astype(BF16)
        n = len(copies)
        copy = pltpu.make_async_copy(buffer.at[rows, :], out.at[rows, :], sems.at[n])
        copy.start()
        copies.append(copy)

    for b in range(half_rows // BLOCK):
        rows = pl.ds(b * BLOCK, BLOCK)
        q, k, v, g = q_ref[rows, :], k_ref[rows, :], v_ref[rows, :], g_ref[rows, :]
        put(qg_in[rows, :] + dot(g, kv_used[b], 1, 1), qg_ref, qg_hbm, rows)
        put(kg_in[rows, :] + dot(v, back_used[b], 1, 1), kg_ref, kg_hbm, rows)
        put(vg_in[rows, :] + dot(k, back_used[b], 1, 0), vg_ref, vg_hbm, rows)
        scaling = scaling_of(start + b * BLOCK, BLOCK, width)
        put((att_in[rows, :] + dot(q, kv_used[b], 1, 0)) * scaling, att_ref, att_hbm, rows)
    for copy in copies:
        copy.wait()


def in_memory(array):
    return pltpu.with_memory_space_constraint(array, pltpu.HBM)


def call(kernel, outs, limit, **options):
    return pl.pallas_call(
        kernel,
        out_shape=outs,
        compiler_params=pltpu.CompilerParams(vmem_limit_bytes=limit),
        **options,
    )


def per_device(groups, queries, key_vectors, value_vectors, out_grad):
    half_rows, width = queries.shape
    blocks = half_rows // BLOCK
    rows16 = jax.ShapeDtypeStruct((half_rows, width), BF16)
    rows32 = jax.ShapeDtypeStruct((half_rows, width), F32)
    states = jax.ShapeDtypeStruct((2 * width, width), F32)
    in_hbm = pl.BlockSpec(memory_space=pltpu.HBM)
    send, keep, q, k, v, grad = call(
        outer_kernel,
        (states, states) + (rows16,) * 4,
        2**23,
        in_specs=[in_hbm] * 4,
        scratch_shapes=[
            pltpu.VMEM((half_rows, width), BF16),
            pltpu.SemaphoreType.DMA((blocks, 4)),
        ],
    )(*(in_memory(x) for x in (queries, key_vectors, value_vectors, out_grad)))
    count = len(groups[0])
    parts = send.reshape(count, 2 * width // count, width)
    parts = lax.all_to_all(parts, AXES, 0, 0, axis_index_groups=groups)
    local = call(
        local_kernel,
        (rows32,) * 4,
        2**24,
        cost_estimate=pl.CostEstimate(
            flops=12 * half_rows * BLOCK * width, bytes_accessed=2**22, transcendentals=0
        ),
    )(q, k, v, grad)
    parts = call(scan_kernel, jax.ShapeDtypeStruct(parts.shape, F32), 2**23)(parts)
    parts = lax.all_to_all(parts, AXES, 0, 0, axis_index_groups=groups)
    state = parts.reshape(2 * width, width)
    return call(
        final_kernel,
        (rows16,) * 4,
        2**24,
        out_specs=(in_hbm,) * 4,
        scratch_shapes=[pltpu.VMEM((half_rows, width), BF16)] * 4
        + [pltpu.SemaphoreType.DMA((4 * blocks,))],
    )(q, k, v, grad, state, keep, *local)


def solution(mesh):
    n_seq, n_inner = mesh.shape["seq"], mesh.shape["inner"]
    groups = [
        [s * n_inner + 2 * h + side for s in range(n_seq) for side in range(2)]
        for h in range(n_inner // 2)
    ]
    spec = P("seq", "inner")
    return jax.shard_map(
        functools.partial(per_device, groups),
        mesh=mesh,
        in_specs=(spec,) * 4,
        out_specs=(spec,) * 4,
        check_vma=False,
    )
```

```python
import functools

import jax
import jax.numpy as jnp
from jax import lax
from jax.experimental import pallas as pl
from jax.experimental.pallas import tpu as pltpu
from jax.sharding import PartitionSpec as P

BLOCK = 512
SUB = 256
AXES = ("seq", "inner")
F32 = jnp.float32
BF16 = jnp.bfloat16


def dot(a, b, ca, cb):
    return lax.dot_general(a, b, (((ca,), (cb,)), ((), ())), preferred_element_type=F32)


def scaling_of(start, rows, width):
    row = lax.broadcasted_iota(jnp.int32, (rows, width), 0)
    position = (start + row).astype(F32)
    return 1.0 / jnp.sqrt(width * (position + 1.0))


def first_position(half_rows):
    return (lax.axis_index("seq") * 2 + lax.axis_index("inner") % 2) * half_rows


def outer_kernel(
    q_hbm, k_hbm, v_hbm, o_hbm,
    send_ref, own_ref, keep_ref, q_ref, k_ref, v_ref, grad_ref,
    o_ref, total_ref, sems,
):
    half_rows, width = q_ref.shape
    start = first_position(half_rows)
    pairs = ((k_hbm, k_ref), (v_hbm, v_ref), (o_hbm, o_ref), (q_hbm, q_ref))
    copies = []
    for b in range(half_rows // BLOCK):
        rows = pl.ds(b * BLOCK, BLOCK)
        for i, (source, target) in enumerate(pairs):
            copies.append(
                pltpu.make_async_copy(source.at[rows, :], target.at[rows, :], sems.at[b, i])
            )
    for copy in copies:
        copy.start()
    kv, back = [], []
    for b in range(half_rows // BLOCK):
        rows = pl.ds(b * BLOCK, BLOCK)
        scaling = scaling_of(start + b * BLOCK, BLOCK, width)
        copies[4 * b].wait()
        copies[4 * b + 1].wait()
        kv.append(dot(k_ref[rows, :], v_ref[rows, :], 0, 0))
        copies[4 * b + 2].wait()
        grad = (scaling * o_ref[rows, :].astype(F32)).astype(BF16)
        grad_ref[rows, :] = grad
        copies[4 * b + 3].wait()
        back.append(dot(q_ref[rows, :], grad, 0, 0))
    keep_ref[:width, :] = kv[0]
    keep_ref[width:, :] = back[1]
    half = width // 2
    mine = lax.axis_index("inner") % 2
    for i, total in enumerate((kv[0] + kv[1], back[0] + back[1])):
        total_ref[...] = total
        own_ref[i] = total_ref[pl.ds(mine * half, half), :]
        send_ref[i] = total_ref[pl.ds((1 - mine) * half, half), :]


def spread_kernel(own_ref, got_ref, *refs):
    out_ref = refs[-1]
    me = lax.axis_index("seq")
    kv = own_ref[0] + got_ref[0]
    back = own_ref[1] + got_ref[1]
    for i in range(out_ref.shape[0]):
        out_ref[i] = jnp.where(i > me, kv, back)


def gather_kernel(parts_ref, own_ref, got_ref, send_ref, mine_ref):
    me = lax.axis_index("seq")
    is_second = lax.axis_index("inner") % 2 == 1
    zero = jnp.zeros(parts_ref.shape[1:], F32)
    earlier, later = zero, zero
    count = parts_ref.shape[0]
    for i in range(count):
        earlier = earlier + jnp.where(i < me, parts_ref[i], zero)
        j = count - 1 - i
        later = later + jnp.where(j > me, parts_ref[j], zero)
    send_ref[0] = earlier + jnp.where(is_second, zero, own_ref[0])
    send_ref[1] = later + jnp.where(is_second, own_ref[1], zero)
    mine_ref[0] = earlier + jnp.where(is_second, got_ref[0], zero)
    mine_ref[1] = later + jnp.where(is_second, zero, got_ref[1])


def local_kernel(b, q_ref, k_ref, v_ref, g_ref, *refs):
    outs = refs[-4:]
    row = lax.broadcasted_iota(jnp.int32, (SUB, SUB), 0)
    col = lax.broadcasted_iota(jnp.int32, (SUB, SUB), 1)
    causal = row >= col
    n = BLOCK // SUB
    tiles = [pl.ds(b * BLOCK + i * SUB, SUB) for i in range(n)]
    q, k, v, g = ([ref[t, :] for t in tiles] for ref in (q_ref, k_ref, v_ref, g_ref))
    att, qg, kg, vg = ([0.0] * n for _ in range(4))
    for i in range(n):
        for j in range(i + 1):
            w = dot(q[i], k[j], 1, 1)
            s = dot(g[i], v[j], 1, 1)
            if i == j:
                w = jnp.where(causal, w, 0.0)
                s = jnp.where(causal, s, 0.0)
            w = w.astype(BF16)
            s = s.astype(BF16)
            att[i] = att[i] + dot(w, v[j], 1, 0)
            qg[i] = qg[i] + dot(s, k[j], 1, 0)
            kg[j] = kg[j] + dot(s, q[i], 0, 0)
            vg[j] = vg[j] + dot(w, g[i], 0, 0)
    for out, parts in zip(outs, (att, qg, kg, vg)):
        for i in range(n):
            out[pl.ds(i * SUB, SUB), :] = parts[i]


def final_kernel(q_ref, k_ref, v_ref, g_ref, mine_ref, got_ref, keep_ref, *refs):
    local, outs = refs[:8], refs[8:12]
    buffers, state_ref, sems = refs[12:16], refs[16], refs[17]
    half_rows, width = q_ref.shape
    start = first_position(half_rows)
    half = width // 2
    mine = lax.axis_index("inner") % 2
    for i in range(2):
        state_ref[i, pl.ds(mine * half, half), :] = mine_ref[i]
        state_ref[i, pl.ds((1 - mine) * half, half), :] = got_ref[i]
    kv0 = state_ref[0]
    back1 = state_ref[1]
    kv_used = [kv0.astype(BF16), (kv0 + keep_ref[:width, :]).astype(BF16)]
    back_used = [(back1 + keep_ref[width:, :]).astype(BF16), back1.astype(BF16)]
    copies = []

    def put(i, value, rows):
        buffers[i][rows, :] = value.astype(BF16)
        copy = pltpu.make_async_copy(
            buffers[i].at[rows, :], outs[i].at[rows, :], sems.at[len(copies)]
        )
        copy.start()
        copies.append(copy)

    for b in range(half_rows // BLOCK):
        rows = pl.ds(b * BLOCK, BLOCK)
        q, k, v, g = q_ref[rows, :], k_ref[rows, :], v_ref[rows, :], g_ref[rows, :]
        att, qg, kg, vg = (ref[...] for ref in local[4 * b : 4 * b + 4])
        put(1, qg + dot(g, kv_used[b], 1, 1), rows)
        put(2, kg + dot(v, back_used[b], 1, 1), rows)
        put(3, vg + dot(k, back_used[b], 1, 0), rows)
        scaling = scaling_of(start + b * BLOCK, BLOCK, width)
        put(0, (att + dot(q, kv_used[b], 1, 0)) * scaling, rows)
    for copy in copies:
        copy.wait()


def in_memory(array):
    return pltpu.with_memory_space_constraint(array, pltpu.HBM)


def call(kernel, outs, limit, **options):
    return pl.pallas_call(
        kernel,
        out_shape=outs,
        compiler_params=pltpu.CompilerParams(vmem_limit_bytes=limit),
        **options,
    )


def per_device(pairs, queries, key_vectors, value_vectors, out_grad):
    half_rows, width = queries.shape
    blocks = half_rows // BLOCK
    rows16 = jax.ShapeDtypeStruct((half_rows, width), BF16)
    block32 = jax.ShapeDtypeStruct((BLOCK, width), F32)
    states = jax.ShapeDtypeStruct((2 * width, width), F32)
    halves = jax.ShapeDtypeStruct((2, width // 2, width), F32)
    in_hbm = pl.BlockSpec(memory_space=pltpu.HBM)
    in_vmem = pl.BlockSpec(memory_space=pltpu.VMEM)
    anywhere = pl.BlockSpec(memory_space=pl.ANY)
    send, own, keep, q, k, v, grad = call(
        outer_kernel,
        (halves, halves, states) + (rows16,) * 4,
        2**23,
        in_specs=[in_hbm] * 4,
        scratch_shapes=[
            pltpu.VMEM((half_rows, width), BF16),
            pltpu.VMEM((width, width), F32),
            pltpu.SemaphoreType.DMA((blocks, 4)),
        ],
    )(*(in_memory(x) for x in (queries, key_vectors, value_vectors, out_grad)))

    def in_block(b, *after):
        return call(
            functools.partial(local_kernel, b),
            (block32,) * 4,
            2**24,
            in_specs=[in_vmem] * 4 + [anywhere] * len(after),
            cost_estimate=pl.CostEstimate(
                flops=12 * BLOCK * BLOCK * width, bytes_accessed=2**21, transcendentals=0
            ),
        )(q, k, v, grad, *after)

    got = lax.ppermute(send, AXES, pairs)
    first = in_block(0)
    count = lax.axis_size("seq")
    parts = call(
        spread_kernel,
        jax.ShapeDtypeStruct((count, width // 2, width), F32),
        2**23,
        in_specs=[in_vmem] * 2 + [anywhere],
    )(own, got, first[0])
    parts = lax.all_to_all(parts, "seq", 0, 0)
    send, mine = call(gather_kernel, (halves,) * 2, 2**23)(parts, own, got)
    got = lax.ppermute(send, AXES, pairs)
    second = in_block(1, mine)
    return call(
        final_kernel,
        (rows16,) * 4,
        2**24,
        out_specs=(in_hbm,) * 4,
        scratch_shapes=[pltpu.VMEM((half_rows, width), BF16)] * 4
        + [pltpu.VMEM((2, width, width), F32), pltpu.SemaphoreType.DMA((4 * blocks,))],
    )(q, k, v, grad, mine, got, keep, *first, *second)


def solution(mesh):
    count = mesh.shape["seq"] * mesh.shape["inner"]
    pairs = [(i, i ^ 1) for i in range(count)]
    spec = P("seq", "inner")
    return jax.shard_map(
        functools.partial(per_device, pairs),
        mesh=mesh,
        in_specs=(spec,) * 4,
        out_specs=(spec,) * 4,
        check_vma=False,
    )
```

```python
import functools

import jax
import jax.numpy as jnp
from jax import lax
from jax.experimental import pallas as pl
from jax.experimental.pallas import tpu as pltpu
from jax.sharding import PartitionSpec as P

BLOCK = 512
SUB = 256
AXES = ("seq", "inner")
F32 = jnp.float32
BF16 = jnp.bfloat16


def dot(a, b, ca, cb):
    return lax.dot_general(a, b, (((ca,), (cb,)), ((), ())), preferred_element_type=F32)


def scaling_of(start, rows, width):
    row = lax.broadcasted_iota(jnp.int32, (rows, width), 0)
    position = (start + row).astype(F32)
    return 1.0 / jnp.sqrt(width * (position + 1.0))


def first_position(half_rows):
    return (lax.axis_index("seq") * 2 + lax.axis_index("inner") % 2) * half_rows


def outer_kernel(
    q_hbm, k_hbm, v_hbm, o_hbm,
    send_ref, own_ref, keep_ref, q_ref, k_ref, v_ref, grad_ref,
    o_ref, total_ref, sems,
):
    half_rows, width = q_ref.shape
    start = first_position(half_rows)
    pairs = ((k_hbm, k_ref), (v_hbm, v_ref), (o_hbm, o_ref), (q_hbm, q_ref))
    copies = []
    for b in range(half_rows // BLOCK):
        rows = pl.ds(b * BLOCK, BLOCK)
        for i, (source, target) in enumerate(pairs):
            copies.append(
                pltpu.make_async_copy(source.at[rows, :], target.at[rows, :], sems.at[b, i])
            )
    for copy in copies:
        copy.start()
    kv, back = [], []
    for b in range(half_rows // BLOCK):
        rows = pl.ds(b * BLOCK, BLOCK)
        scaling = scaling_of(start + b * BLOCK, BLOCK, width)
        copies[4 * b].wait()
        copies[4 * b + 1].wait()
        kv.append(dot(k_ref[rows, :], v_ref[rows, :], 0, 0))
        copies[4 * b + 2].wait()
        grad = (scaling * o_ref[rows, :].astype(F32)).astype(BF16)
        grad_ref[rows, :] = grad
        copies[4 * b + 3].wait()
        back.append(dot(q_ref[rows, :], grad, 0, 0))
    keep_ref[:width, :] = kv[0]
    keep_ref[width:, :] = back[1]
    half = width // 2
    side = lax.axis_index("inner") % 2
    total_ref[0] = kv[0] + kv[1]
    total_ref[1] = back[0] + back[1]
    own_ref[0] = total_ref[0, pl.ds(side * half, half), :]
    own_ref[1] = total_ref[1, pl.ds(side * half, half), :]
    send_ref[:width, :] = total_ref[side]
    send_ref[width:, :] = total_ref[1 - side, pl.ds((1 - side) * half, half), :]


def spread_kernel(own_ref, got_ref, *refs):
    out_ref = refs[-1]
    count, rows, width = out_ref.shape
    half = width // 2
    me = lax.axis_index("seq")
    side = lax.axis_index("inner") % 2
    whole = got_ref[pl.ds(side * half, half), :]
    part = got_ref[width:, :]
    kv = own_ref[0] + jnp.where(side == 0, part, whole)
    back = own_ref[1] + jnp.where(side == 0, whole, part)
    for i in range(count):
        takes_kv = jnp.logical_or(i // 2 > me // 2, (i // 2 == me // 2) & (me % 2 == 0))
        cut = slice((i % 2) * rows, (i % 2 + 1) * rows)
        out_ref[i] = jnp.where(takes_kv, kv[cut], back[cut])


def gather_kernel(parts_ref, send_ref):
    pair = lax.axis_index("seq") // 2
    zero = jnp.zeros(parts_ref.shape[1:], F32)
    earlier, later = zero, zero
    count = parts_ref.shape[0]
    for i in range(count):
        earlier = earlier + jnp.where(i // 2 < pair, parts_ref[i], zero)
        j = count - 1 - i
        later = later + jnp.where(j // 2 > pair, parts_ref[j], zero)
    with_first = earlier + parts_ref[2 * pair]
    with_second = later + parts_ref[2 * pair + 1]
    for side in range(2):
        send_ref[side, 0] = earlier
        send_ref[side, 1] = with_second
        send_ref[2 + side, 0] = with_first
        send_ref[2 + side, 1] = later


def local_kernel(b, q_ref, k_ref, v_ref, g_ref, *refs):
    outs = refs[-4:]
    row = lax.broadcasted_iota(jnp.int32, (SUB, SUB), 0)
    col = lax.broadcasted_iota(jnp.int32, (SUB, SUB), 1)
    causal = row >= col
    n = BLOCK // SUB
    tiles = [pl.ds(b * BLOCK + i * SUB, SUB) for i in range(n)]
    q, k, v, g = ([ref[t, :] for t in tiles] for ref in (q_ref, k_ref, v_ref, g_ref))
    att, qg, kg, vg = ([0.0] * n for _ in range(4))
    for i in range(n):
        for j in range(i + 1):
            w = dot(q[i], k[j], 1, 1)
            s = dot(g[i], v[j], 1, 1)
            if i == j:
                w = jnp.where(causal, w, 0.0)
                s = jnp.where(causal, s, 0.0)
            w = w.astype(BF16)
            s = s.astype(BF16)
            att[i] = att[i] + dot(w, v[j], 1, 0)
            qg[i] = qg[i] + dot(s, k[j], 1, 0)
            kg[j] = kg[j] + dot(s, q[i], 0, 0)
            vg[j] = vg[j] + dot(w, g[i], 0, 0)
    for out, parts in zip(outs, (att, qg, kg, vg)):
        for i in range(n):
            out[pl.ds(i * SUB, SUB), :] = parts[i]


def final_kernel(q_ref, k_ref, v_ref, g_ref, state_ref, got_ref, keep_ref, *refs):
    local, outs = refs[:8], refs[8:12]
    buffers, sems = refs[12:16], refs[16]
    half_rows, width = q_ref.shape
    start = first_position(half_rows)
    is_second = lax.axis_index("inner") % 2 == 1
    kv0, back1 = (
        jnp.concatenate([state_ref[2 * z + c, i] for c in range(2) for z in range(2)], 0)
        for i in range(2)
    )
    other = got_ref[:width, :]
    kv0 = kv0 + jnp.where(is_second, other, 0.0)
    back1 = back1 + jnp.where(is_second, 0.0, other)
    kv_used = [kv0.astype(BF16), (kv0 + keep_ref[:width, :]).astype(BF16)]
    back_used = [(back1 + keep_ref[width:, :]).astype(BF16), back1.astype(BF16)]
    copies = []

    def put(i, value, rows):
        buffers[i][rows, :] = value.astype(BF16)
        copy = pltpu.make_async_copy(
            buffers[i].at[rows, :], outs[i].at[rows, :], sems.at[len(copies)]
        )
        copy.start()
        copies.append(copy)

    for b in range(half_rows // BLOCK):
        rows = pl.ds(b * BLOCK, BLOCK)
        q, k, v, g = q_ref[rows, :], k_ref[rows, :], v_ref[rows, :], g_ref[rows, :]
        att, qg, kg, vg = (ref[...] for ref in local[4 * b : 4 * b + 4])
        put(1, qg + dot(g, kv_used[b], 1, 1), rows)
        put(2, kg + dot(v, back_used[b], 1, 1), rows)
        put(3, vg + dot(k, back_used[b], 1, 0), rows)
        scaling = scaling_of(start + b * BLOCK, BLOCK, width)
        put(0, (att + dot(q, kv_used[b], 1, 0)) * scaling, rows)
    for copy in copies:
        copy.wait()


def in_memory(array):
    return pltpu.with_memory_space_constraint(array, pltpu.HBM)


def call(kernel, outs, limit, **options):
    return pl.pallas_call(
        kernel,
        out_shape=outs,
        compiler_params=pltpu.CompilerParams(vmem_limit_bytes=limit),
        **options,
    )


def per_device(pairs, groups, queries, key_vectors, value_vectors, out_grad):
    half_rows, width = queries.shape
    blocks = half_rows // BLOCK
    rows16 = jax.ShapeDtypeStruct((half_rows, width), BF16)
    block32 = jax.ShapeDtypeStruct((BLOCK, width), F32)
    states = jax.ShapeDtypeStruct((2 * width, width), F32)
    half = width // 2
    halves = jax.ShapeDtypeStruct((2, half, width), F32)
    sent = jax.ShapeDtypeStruct((width + half, width), F32)
    in_hbm = pl.BlockSpec(memory_space=pltpu.HBM)
    in_vmem = pl.BlockSpec(memory_space=pltpu.VMEM)
    anywhere = pl.BlockSpec(memory_space=pl.ANY)
    send, own, keep, q, k, v, grad = call(
        outer_kernel,
        (sent, halves, states) + (rows16,) * 4,
        2**23,
        in_specs=[in_hbm] * 4,
        scratch_shapes=[
            pltpu.VMEM((half_rows, width), BF16),
            pltpu.VMEM((2, width, width), F32),
            pltpu.SemaphoreType.DMA((blocks, 4)),
        ],
    )(*(in_memory(x) for x in (queries, key_vectors, value_vectors, out_grad)))

    def in_block(b, *after):
        return call(
            functools.partial(local_kernel, b),
            (block32,) * 4,
            2**24,
            in_specs=[in_vmem] * 4 + [anywhere] * len(after),
            cost_estimate=pl.CostEstimate(
                flops=12 * BLOCK * BLOCK * width, bytes_accessed=2**21, transcendentals=0
            ),
        )(q, k, v, grad, *after)

    got = lax.ppermute(send, AXES, pairs)
    first = in_block(0)
    count = lax.axis_size("seq")
    quarter = half // 2
    parts = call(
        spread_kernel,
        jax.ShapeDtypeStruct((count, quarter, width), F32),
        2**23,
        in_specs=[in_vmem] * 2 + [anywhere],
    )(own, got, first[0])
    parts = lax.all_to_all(parts, "seq", 0, 0)
    quads = jax.ShapeDtypeStruct((4, 2, quarter, width), F32)
    state = call(gather_kernel, quads, 2**23)(parts)
    second = in_block(1, state)
    state = lax.all_to_all(state, AXES, 0, 0, axis_index_groups=groups)
    return call(
        final_kernel,
        (rows16,) * 4,
        2**24,
        out_specs=(in_hbm,) * 4,
        scratch_shapes=[pltpu.VMEM((half_rows, width), BF16)] * 4
        + [pltpu.SemaphoreType.DMA((4 * blocks,))],
    )(q, k, v, grad, state, got, keep, *first, *second)


def solution(mesh):
    n_seq, n_inner = mesh.shape["seq"], mesh.shape["inner"]
    pairs = [(i, i ^ 1) for i in range(n_seq * n_inner)]
    groups = [
        [(2 * x + z) * n_inner + 2 * h + side for z in range(2) for side in range(2)]
        for x in range(n_seq // 2)
        for h in range(n_inner // 2)
    ]
    spec = P("seq", "inner")
    return jax.shard_map(
        functools.partial(per_device, pairs, groups),
        mesh=mesh,
        in_specs=(spec,) * 4,
        out_specs=(spec,) * 4,
        check_vma=False,
    )
```

```python
import functools

import jax
import jax.numpy as jnp
from jax import lax
from jax.experimental import pallas as pl
from jax.experimental.pallas import tpu as pltpu
from jax.sharding import PartitionSpec as P

BLOCK = 512
SUB = 256
AXES = ("seq", "inner")
F32 = jnp.float32
BF16 = jnp.bfloat16


def dot(a, b, ca, cb):
    return lax.dot_general(a, b, (((ca,), (cb,)), ((), ())), preferred_element_type=F32)


def scaling_of(start, rows, width):
    row = lax.broadcasted_iota(jnp.int32, (rows, width), 0)
    position = (start + row).astype(F32)
    return 1.0 / jnp.sqrt(width * (position + 1.0))


def first_position(half_rows):
    return (lax.axis_index("seq") * 2 + lax.axis_index("inner") % 2) * half_rows


def outer_kernel(
    q_hbm, k_hbm, v_hbm, o_hbm,
    send_ref, own_ref, keep_ref, q_ref, k_ref, v_ref, grad_ref,
    o_ref, total_ref, sems,
):
    half_rows, width = q_ref.shape
    start = first_position(half_rows)
    pairs = ((k_hbm, k_ref), (v_hbm, v_ref), (o_hbm, o_ref), (q_hbm, q_ref))
    copies = []
    for b in range(half_rows // BLOCK):
        rows = pl.ds(b * BLOCK, BLOCK)
        for i, (source, target) in enumerate(pairs):
            copies.append(
                pltpu.make_async_copy(source.at[rows, :], target.at[rows, :], sems.at[b, i])
            )
    for copy in copies:
        copy.start()
    kv, back = [], []
    for b in range(half_rows // BLOCK):
        rows = pl.ds(b * BLOCK, BLOCK)
        scaling = scaling_of(start + b * BLOCK, BLOCK, width)
        copies[4 * b].wait()
        copies[4 * b + 1].wait()
        kv.append(dot(k_ref[rows, :], v_ref[rows, :], 0, 0))
        copies[4 * b + 2].wait()
        grad = (scaling * o_ref[rows, :].astype(F32)).astype(BF16)
        grad_ref[rows, :] = grad
        copies[4 * b + 3].wait()
        back.append(dot(q_ref[rows, :], grad, 0, 0))
    keep_ref[:width, :] = kv[0]
    keep_ref[width:, :] = back[1]
    half = width // 2
    side = lax.axis_index("inner") % 2
    total_ref[0] = kv[0] + kv[1]
    total_ref[1] = back[0] + back[1]
    own_ref[0] = total_ref[0, pl.ds(side * half, half), :]
    own_ref[1] = total_ref[1, pl.ds(side * half, half), :]
    send_ref[:width, :] = total_ref[side]
    send_ref[width:, :] = total_ref[1 - side, pl.ds((1 - side) * half, half), :]


def spread_kernel(own_ref, got_ref, *refs):
    out_ref = refs[-1]
    count, rows, width = out_ref.shape
    half = width // 2
    me = lax.axis_index("seq")
    side = lax.axis_index("inner") % 2
    whole = got_ref[pl.ds(side * half, half), :]
    part = got_ref[width:, :]
    kv = own_ref[0] + jnp.where(side == 0, part, whole)
    back = own_ref[1] + jnp.where(side == 0, whole, part)
    for i in range(count):
        takes_kv = jnp.logical_or(i // 2 > me // 2, (i // 2 == me // 2) & (me % 2 == 0))
        cut = slice((i % 2) * rows, (i % 2 + 1) * rows)
        out_ref[i] = jnp.where(takes_kv, kv[cut], back[cut])


def gather_kernel(parts_ref, send_ref):
    pair = lax.axis_index("seq") // 2
    zero = jnp.zeros(parts_ref.shape[1:], F32)
    earlier, later = zero, zero
    count = parts_ref.shape[0]
    for i in range(count):
        earlier = earlier + jnp.where(i // 2 < pair, parts_ref[i], zero)
        j = count - 1 - i
        later = later + jnp.where(j // 2 > pair, parts_ref[j], zero)
    with_first = earlier + parts_ref[2 * pair]
    with_second = later + parts_ref[2 * pair + 1]
    for side in range(2):
        send_ref[side, 0] = earlier
        send_ref[side, 1] = with_second
        send_ref[2 + side, 0] = with_first
        send_ref[2 + side, 1] = later


def local_kernel(q_ref, k_ref, v_ref, g_ref, att_ref, qg_ref, kg_ref, vg_ref):
    row = lax.broadcasted_iota(jnp.int32, (SUB, SUB), 0)
    col = lax.broadcasted_iota(jnp.int32, (SUB, SUB), 1)
    causal = row >= col
    n = BLOCK // SUB

    def masked(scores):
        left = scores.shape[1] - SUB
        last = jnp.where(causal, scores[:, left:], 0.0)
        if left:
            last = jnp.concatenate([scores[:, :left], last], 1)
        return last.astype(BF16)

    for b in range(q_ref.shape[0] // BLOCK):
        weights, scores = [], []
        for i in range(n):
            own = pl.ds(b * BLOCK + i * SUB, SUB)
            before = pl.ds(b * BLOCK, (i + 1) * SUB)
            weights.append(masked(dot(q_ref[own, :], k_ref[before, :], 1, 1)))
            scores.append(masked(dot(g_ref[own, :], v_ref[before, :], 1, 1)))
            att_ref[own, :] = dot(weights[i], v_ref[before, :], 1, 0)
            qg_ref[own, :] = dot(scores[i], k_ref[before, :], 1, 0)
        for j in range(n):
            own = pl.ds(b * BLOCK + j * SUB, SUB)
            after = pl.ds(b * BLOCK + j * SUB, (n - j) * SUB)
            cut = slice(j * SUB, (j + 1) * SUB)
            w = jnp.concatenate([weights[i][:, cut] for i in range(j, n)], 0)
            s = jnp.concatenate([scores[i][:, cut] for i in range(j, n)], 0)
            vg_ref[own, :] = dot(w, g_ref[after, :], 0, 0)
            kg_ref[own, :] = dot(s, q_ref[after, :], 0, 0)


def final_kernel(q_ref, k_ref, v_ref, g_ref, state_ref, got_ref, keep_ref, *refs):
    local, outs = refs[:4], refs[4:8]
    buffers, sems = refs[8:12], refs[12]
    half_rows, width = q_ref.shape
    start = first_position(half_rows)
    is_second = lax.axis_index("inner") % 2 == 1
    kv0, back1 = (
        jnp.concatenate([state_ref[2 * z + c, i] for c in range(2) for z in range(2)], 0)
        for i in range(2)
    )
    other = got_ref[:width, :]
    kv0 = kv0 + jnp.where(is_second, other, 0.0)
    back1 = back1 + jnp.where(is_second, 0.0, other)
    kv_used = [kv0.astype(BF16), (kv0 + keep_ref[:width, :]).astype(BF16)]
    back_used = [(back1 + keep_ref[width:, :]).astype(BF16), back1.astype(BF16)]
    copies = []

    def put(i, value, rows):
        buffers[i][rows, :] = value.astype(BF16)
        copy = pltpu.make_async_copy(
            buffers[i].at[rows, :], outs[i].at[rows, :], sems.at[len(copies)]
        )
        copy.start()
        copies.append(copy)

    for b in range(half_rows // BLOCK):
        rows = pl.ds(b * BLOCK, BLOCK)
        q, k, v, g = q_ref[rows, :], k_ref[rows, :], v_ref[rows, :], g_ref[rows, :]
        att, qg, kg, vg = (ref[rows, :] for ref in local)
        put(1, qg + dot(g, kv_used[b], 1, 1), rows)
        put(2, kg + dot(v, back_used[b], 1, 1), rows)
        put(3, vg + dot(k, back_used[b], 1, 0), rows)
        scaling = scaling_of(start + b * BLOCK, BLOCK, width)
        put(0, (att + dot(q, kv_used[b], 1, 0)) * scaling, rows)
    for copy in copies:
        copy.wait()


def in_memory(array):
    return pltpu.with_memory_space_constraint(array, pltpu.HBM)


def call(kernel, outs, limit, **options):
    return pl.pallas_call(
        kernel,
        out_shape=outs,
        compiler_params=pltpu.CompilerParams(vmem_limit_bytes=limit),
        **options,
    )


def per_device(pairs, groups, queries, key_vectors, value_vectors, out_grad):
    half_rows, width = queries.shape
    blocks = half_rows // BLOCK
    rows16 = jax.ShapeDtypeStruct((half_rows, width), BF16)
    rows32 = jax.ShapeDtypeStruct((half_rows, width), F32)
    states = jax.ShapeDtypeStruct((2 * width, width), F32)
    half = width // 2
    halves = jax.ShapeDtypeStruct((2, half, width), F32)
    sent = jax.ShapeDtypeStruct((width + half, width), F32)
    in_hbm = pl.BlockSpec(memory_space=pltpu.HBM)
    in_vmem = pl.BlockSpec(memory_space=pltpu.VMEM)
    anywhere = pl.BlockSpec(memory_space=pl.ANY)
    send, own, keep, q, k, v, grad = call(
        outer_kernel,
        (sent, halves, states) + (rows16,) * 4,
        2**23,
        in_specs=[in_hbm] * 4,
        scratch_shapes=[
            pltpu.VMEM((half_rows, width), BF16),
            pltpu.VMEM((2, width, width), F32),
            pltpu.SemaphoreType.DMA((blocks, 4)),
        ],
    )(*(in_memory(x) for x in (queries, key_vectors, value_vectors, out_grad)))

    got = lax.ppermute(send, AXES, pairs)
    local = call(
        local_kernel,
        (rows32,) * 4,
        2**24,
        cost_estimate=pl.CostEstimate(
            flops=12 * half_rows * BLOCK * width, bytes_accessed=2**22, transcendentals=0
        ),
    )(q, k, v, grad)
    count = lax.axis_size("seq")
    quarter = half // 2
    parts = call(
        spread_kernel,
        jax.ShapeDtypeStruct((count, quarter, width), F32),
        2**23,
        in_specs=[in_vmem] * 2 + [anywhere],
    )(own, got, local[0])
    parts = lax.all_to_all(parts, "seq", 0, 0)
    quads = jax.ShapeDtypeStruct((4, 2, quarter, width), F32)
    state = call(gather_kernel, quads, 2**23)(parts)
    state = lax.all_to_all(state, AXES, 0, 0, axis_index_groups=groups)
    return call(
        final_kernel,
        (rows16,) * 4,
        2**24,
        out_specs=(in_hbm,) * 4,
        scratch_shapes=[pltpu.VMEM((half_rows, width), BF16)] * 4
        + [pltpu.SemaphoreType.DMA((4 * blocks,))],
    )(q, k, v, grad, state, got, keep, *local)


def solution(mesh):
    n_seq, n_inner = mesh.shape["seq"], mesh.shape["inner"]
    pairs = [(i, i ^ 1) for i in range(n_seq * n_inner)]
    groups = [
        [(2 * x + z) * n_inner + 2 * h + side for z in range(2) for side in range(2)]
        for x in range(n_seq // 2)
        for h in range(n_inner // 2)
    ]
    spec = P("seq", "inner")
    return jax.shard_map(
        functools.partial(per_device, pairs, groups),
        mesh=mesh,
        in_specs=(spec,) * 4,
        out_specs=(spec,) * 4,
        check_vma=False,
    )
```

```python
import functools

import jax
import jax.numpy as jnp
from jax import lax
from jax.experimental import pallas as pl
from jax.experimental.pallas import tpu as pltpu
from jax.sharding import PartitionSpec as P

BLOCK = 512
SUB = 256
AXES = ("seq", "inner")
F32 = jnp.float32
BF16 = jnp.bfloat16


def dot(a, b, ca, cb):
    return lax.dot_general(a, b, (((ca,), (cb,)), ((), ())), preferred_element_type=F32)


def scaling_of(start, rows, width):
    row = lax.broadcasted_iota(jnp.int32, (rows, width), 0)
    position = (start + row).astype(F32)
    return lax.rsqrt(width * (position + 1.0))


def first_position(half_rows):
    return (lax.axis_index("seq") * 2 + lax.axis_index("inner") % 2) * half_rows


def outer_kernel(
    q_hbm, k_hbm, v_hbm, o_hbm,
    send_ref, own_ref, keep_ref, q_ref, k_ref, v_ref, grad_ref, scale_ref,
    o_ref, total_ref, sems,
):
    half_rows, width = q_ref.shape
    start = first_position(half_rows)
    pairs = ((k_hbm, k_ref), (v_hbm, v_ref), (o_hbm, o_ref), (q_hbm, q_ref))
    copies = [
        pltpu.make_async_copy(source, target, sems.at[i])
        for i, (source, target) in enumerate(pairs)
    ]
    for copy in copies:
        copy.start()
    scale_ref[...] = scaling_of(start, half_rows, width)
    for copy in copies:
        copy.wait()
    kv, back = [], []
    for b in range(half_rows // BLOCK):
        rows = pl.ds(b * BLOCK, BLOCK)
        grad = (scale_ref[rows, :] * o_ref[rows, :].astype(F32)).astype(BF16)
        grad_ref[rows, :] = grad
        kv.append(dot(k_ref[rows, :], v_ref[rows, :], 0, 0))
        back.append(dot(q_ref[rows, :], grad, 0, 0))
    keep_ref[:width, :] = kv[0]
    keep_ref[width:, :] = back[1]
    half = width // 2
    side = lax.axis_index("inner") % 2
    total_ref[0] = kv[0] + kv[1]
    total_ref[1] = back[0] + back[1]
    own_ref[0] = total_ref[0, pl.ds(side * half, half), :]
    own_ref[1] = total_ref[1, pl.ds(side * half, half), :]
    send_ref[:width, :] = total_ref[side]
    send_ref[width:, :] = total_ref[1 - side, pl.ds((1 - side) * half, half), :]


def spread_kernel(own_ref, got_ref, *refs):
    out_ref = refs[-1]
    count, rows, width = out_ref.shape
    half = width // 2
    me = lax.axis_index("seq")
    side = lax.axis_index("inner") % 2
    whole = got_ref[pl.ds(side * half, half), :]
    part = got_ref[width:, :]
    kv = own_ref[0] + jnp.where(side == 0, part, whole)
    back = own_ref[1] + jnp.where(side == 0, whole, part)
    for i in range(count):
        takes_kv = jnp.logical_or(i // 2 > me // 2, (i // 2 == me // 2) & (me % 2 == 0))
        cut = slice((i % 2) * rows, (i % 2 + 1) * rows)
        out_ref[i] = jnp.where(takes_kv, kv[cut], back[cut])


def gather_kernel(parts_ref, send_ref):
    pair = lax.axis_index("seq") // 2
    zero = jnp.zeros(parts_ref.shape[1:], F32)
    earlier, later = zero, zero
    count = parts_ref.shape[0]
    for i in range(count):
        earlier = earlier + jnp.where(i // 2 < pair, parts_ref[i], zero)
        j = count - 1 - i
        later = later + jnp.where(j // 2 > pair, parts_ref[j], zero)
    with_first = earlier + parts_ref[2 * pair]
    with_second = later + parts_ref[2 * pair + 1]
    for side in range(2):
        send_ref[side, 0] = earlier
        send_ref[side, 1] = with_second
        send_ref[2 + side, 0] = with_first
        send_ref[2 + side, 1] = later


def local_kernel(q_ref, k_ref, v_ref, g_ref, att_ref, qg_ref, kg_ref, vg_ref):
    row = lax.broadcasted_iota(jnp.int32, (SUB, SUB), 0)
    col = lax.broadcasted_iota(jnp.int32, (SUB, SUB), 1)
    causal = row >= col
    n = BLOCK // SUB

    def masked(scores):
        left = scores.shape[1] - SUB
        last = jnp.where(causal, scores[:, left:], 0.0)
        if left:
            last = jnp.concatenate([scores[:, :left], last], 1)
        return last.astype(BF16)

    for b in range(q_ref.shape[0] // BLOCK):
        weights, scores = [], []
        for i in range(n):
            own = pl.ds(b * BLOCK + i * SUB, SUB)
            before = pl.ds(b * BLOCK, (i + 1) * SUB)
            weights.append(masked(dot(q_ref[own, :], k_ref[before, :], 1, 1)))
            scores.append(masked(dot(g_ref[own, :], v_ref[before, :], 1, 1)))
            att_ref[own, :] = dot(weights[i], v_ref[before, :], 1, 0)
            qg_ref[own, :] = dot(scores[i], k_ref[before, :], 1, 0)
        for j in range(n):
            own = pl.ds(b * BLOCK + j * SUB, SUB)
            after = pl.ds(b * BLOCK + j * SUB, (n - j) * SUB)
            cut = slice(j * SUB, (j + 1) * SUB)
            w = jnp.concatenate([weights[i][:, cut] for i in range(j, n)], 0)
            s = jnp.concatenate([scores[i][:, cut] for i in range(j, n)], 0)
            vg_ref[own, :] = dot(w, g_ref[after, :], 0, 0)
            kg_ref[own, :] = dot(s, q_ref[after, :], 0, 0)


def final_kernel(
    q_ref, k_ref, v_ref, g_ref, scale_ref, state_ref, got_ref, keep_ref, *refs
):
    local, outs = refs[:4], refs[4:8]
    buffers, sems = refs[8:12], refs[12]
    half_rows, width = q_ref.shape
    is_second = lax.axis_index("inner") % 2 == 1
    kv0, back1 = (
        jnp.concatenate([state_ref[2 * z + c, i] for c in range(2) for z in range(2)], 0)
        for i in range(2)
    )
    other = got_ref[:width, :]
    kv0 = kv0 + jnp.where(is_second, other, 0.0)
    back1 = back1 + jnp.where(is_second, 0.0, other)
    kv_used = [kv0.astype(BF16), (kv0 + keep_ref[:width, :]).astype(BF16)]
    back_used = [(back1 + keep_ref[width:, :]).astype(BF16), back1.astype(BF16)]
    copies = []

    def put(i, value, rows):
        buffers[i][rows, :] = value.astype(BF16)
        copy = pltpu.make_async_copy(
            buffers[i].at[rows, :], outs[i].at[rows, :], sems.at[len(copies)]
        )
        copy.start()
        copies.append(copy)

    for b in range(half_rows // BLOCK):
        rows = pl.ds(b * BLOCK, BLOCK)
        q, k, v, g = q_ref[rows, :], k_ref[rows, :], v_ref[rows, :], g_ref[rows, :]
        att, qg, kg, vg = (ref[rows, :] for ref in local)
        put(1, qg + dot(g, kv_used[b], 1, 1), rows)
        put(2, kg + dot(v, back_used[b], 1, 1), rows)
        put(3, vg + dot(k, back_used[b], 1, 0), rows)
        put(0, (att + dot(q, kv_used[b], 1, 0)) * scale_ref[rows, :], rows)
    for copy in copies:
        copy.wait()


def in_memory(array):
    return pltpu.with_memory_space_constraint(array, pltpu.HBM)


def call(kernel, outs, limit, **options):
    return pl.pallas_call(
        kernel,
        out_shape=outs,
        compiler_params=pltpu.CompilerParams(vmem_limit_bytes=limit),
        **options,
    )


def per_device(pairs, groups, queries, key_vectors, value_vectors, out_grad):
    half_rows, width = queries.shape
    blocks = half_rows // BLOCK
    rows16 = jax.ShapeDtypeStruct((half_rows, width), BF16)
    rows32 = jax.ShapeDtypeStruct((half_rows, width), F32)
    states = jax.ShapeDtypeStruct((2 * width, width), F32)
    half = width // 2
    halves = jax.ShapeDtypeStruct((2, half, width), F32)
    sent = jax.ShapeDtypeStruct((width + half, width), F32)
    in_hbm = pl.BlockSpec(memory_space=pltpu.HBM)
    in_vmem = pl.BlockSpec(memory_space=pltpu.VMEM)
    anywhere = pl.BlockSpec(memory_space=pl.ANY)
    send, own, keep, q, k, v, grad, scale = call(
        outer_kernel,
        (sent, halves, states) + (rows16,) * 4 + (rows32,),
        2**23,
        in_specs=[in_hbm] * 4,
        scratch_shapes=[
            pltpu.VMEM((half_rows, width), BF16),
            pltpu.VMEM((2, width, width), F32),
            pltpu.SemaphoreType.DMA((4,)),
        ],
    )(*(in_memory(x) for x in (queries, key_vectors, value_vectors, out_grad)))

    got = lax.ppermute(send, AXES, pairs)
    local = call(
        local_kernel,
        (rows32,) * 4,
        2**24,
        cost_estimate=pl.CostEstimate(
            flops=12 * half_rows * BLOCK * width, bytes_accessed=2**22, transcendentals=0
        ),
    )(q, k, v, grad)
    count = lax.axis_size("seq")
    quarter = half // 2
    parts = call(
        spread_kernel,
        jax.ShapeDtypeStruct((count, quarter, width), F32),
        2**23,
        in_specs=[in_vmem] * 2 + [anywhere],
    )(own, got, local[0])
    parts = lax.all_to_all(parts, "seq", 0, 0)
    quads = jax.ShapeDtypeStruct((4, 2, quarter, width), F32)
    state = call(gather_kernel, quads, 2**23)(parts)
    state = lax.all_to_all(state, AXES, 0, 0, axis_index_groups=groups)
    return call(
        final_kernel,
        (rows16,) * 4,
        2**24,
        out_specs=(in_hbm,) * 4,
        scratch_shapes=[pltpu.VMEM((half_rows, width), BF16)] * 4
        + [pltpu.SemaphoreType.DMA((4 * blocks,))],
    )(q, k, v, grad, scale, state, got, keep, *local)


def solution(mesh):
    n_seq, n_inner = mesh.shape["seq"], mesh.shape["inner"]
    pairs = [(i, i ^ 1) for i in range(n_seq * n_inner)]
    groups = [
        [(2 * x + z) * n_inner + 2 * h + side for z in range(2) for side in range(2)]
        for x in range(n_seq // 2)
        for h in range(n_inner // 2)
    ]
    spec = P("seq", "inner")
    return jax.shard_map(
        functools.partial(per_device, pairs, groups),
        mesh=mesh,
        in_specs=(spec,) * 4,
        out_specs=(spec,) * 4,
        check_vma=False,
    )
```

```python
import functools

import jax
import jax.numpy as jnp
from jax import lax
from jax.experimental import pallas as pl
from jax.experimental.pallas import tpu as pltpu
from jax.sharding import PartitionSpec as P

CHUNK = 256
AXES = ("seq", "inner")
F32 = jnp.float32
BF16 = jnp.bfloat16


def dot(a, b, ca, cb):
    return lax.dot_general(a, b, (((ca,), (cb,)), ((), ())), preferred_element_type=F32)


def scaling_of(start, rows, width):
    row = lax.broadcasted_iota(jnp.int32, (rows, width), 0)
    position = (start + row).astype(F32)
    return lax.rsqrt(width * (position + 1.0))


def first_position(half_rows):
    return (lax.axis_index("seq") * 2 + lax.axis_index("inner") % 2) * half_rows


def outer_kernel(
    q_hbm, k_hbm, v_hbm, o_hbm,
    send_ref, own_ref, keep_ref, q_ref, k_ref, v_ref, grad_ref, scale_ref,
    o_ref, total_ref, sems,
):
    half_rows, width = q_ref.shape
    start = first_position(half_rows)
    pairs = ((k_hbm, k_ref), (v_hbm, v_ref), (o_hbm, o_ref), (q_hbm, q_ref))
    copies = [
        pltpu.make_async_copy(source, target, sems.at[i])
        for i, (source, target) in enumerate(pairs)
    ]
    for copy in copies:
        copy.start()
    scale_ref[...] = scaling_of(start, half_rows, width)
    for copy in copies:
        copy.wait()
    kv_total, back_total = 0.0, 0.0
    for c in range(half_rows // CHUNK):
        rows = pl.ds(c * CHUNK, CHUNK)
        grad = (scale_ref[rows, :] * o_ref[rows, :].astype(F32)).astype(BF16)
        grad_ref[rows, :] = grad
        kv = dot(k_ref[rows, :], v_ref[rows, :], 0, 0)
        back = dot(q_ref[rows, :], grad, 0, 0)
        keep_ref[0, c] = kv
        keep_ref[1, c] = back
        kv_total = kv_total + kv
        back_total = back_total + back
    half = width // 2
    side = lax.axis_index("inner") % 2
    total_ref[0] = kv_total
    total_ref[1] = back_total
    own_ref[0] = total_ref[0, pl.ds(side * half, half), :]
    own_ref[1] = total_ref[1, pl.ds(side * half, half), :]
    send_ref[:width, :] = total_ref[side]
    send_ref[width:, :] = total_ref[1 - side, pl.ds((1 - side) * half, half), :]


def spread_kernel(own_ref, got_ref, *refs):
    out_ref = refs[-1]
    count, rows, width = out_ref.shape
    half = width // 2
    me = lax.axis_index("seq")
    side = lax.axis_index("inner") % 2
    whole = got_ref[pl.ds(side * half, half), :]
    part = got_ref[width:, :]
    kv = own_ref[0] + jnp.where(side == 0, part, whole)
    back = own_ref[1] + jnp.where(side == 0, whole, part)
    for i in range(count):
        takes_kv = jnp.logical_or(i // 2 > me // 2, (i // 2 == me // 2) & (me % 2 == 0))
        cut = slice((i % 2) * rows, (i % 2 + 1) * rows)
        out_ref[i] = jnp.where(takes_kv, kv[cut], back[cut])


def gather_kernel(parts_ref, send_ref):
    pair = lax.axis_index("seq") // 2
    zero = jnp.zeros(parts_ref.shape[1:], F32)
    earlier, later = zero, zero
    count = parts_ref.shape[0]
    for i in range(count):
        earlier = earlier + jnp.where(i // 2 < pair, parts_ref[i], zero)
        j = count - 1 - i
        later = later + jnp.where(j // 2 > pair, parts_ref[j], zero)
    with_first = earlier + parts_ref[2 * pair]
    with_second = later + parts_ref[2 * pair + 1]
    for side in range(2):
        send_ref[side, 0] = earlier
        send_ref[side, 1] = with_second
        send_ref[2 + side, 0] = with_first
        send_ref[2 + side, 1] = later


def local_kernel(q_ref, k_ref, v_ref, g_ref, att_ref, qg_ref, kg_ref, vg_ref):
    row = lax.broadcasted_iota(jnp.int32, (CHUNK, CHUNK), 0)
    col = lax.broadcasted_iota(jnp.int32, (CHUNK, CHUNK), 1)
    causal = row >= col
    for c in range(q_ref.shape[0] // CHUNK):
        rows = pl.ds(c * CHUNK, CHUNK)
        q, k, v, g = q_ref[rows, :], k_ref[rows, :], v_ref[rows, :], g_ref[rows, :]
        w = jnp.where(causal, dot(q, k, 1, 1), 0.0).astype(BF16)
        s = jnp.where(causal, dot(g, v, 1, 1), 0.0).astype(BF16)
        att_ref[rows, :] = dot(w, v, 1, 0)
        qg_ref[rows, :] = dot(s, k, 1, 0)
        vg_ref[rows, :] = dot(w, g, 0, 0)
        kg_ref[rows, :] = dot(s, q, 0, 0)


def final_kernel(
    q_ref, k_ref, v_ref, g_ref, scale_ref, state_ref, got_ref, keep_ref, *refs
):
    local, outs = refs[:4], refs[4:8]
    buffers, sems = refs[8:12], refs[12]
    half_rows, width = q_ref.shape
    is_second = lax.axis_index("inner") % 2 == 1
    kv0, back1 = (
        jnp.concatenate([state_ref[2 * z + c, i] for c in range(2) for z in range(2)], 0)
        for i in range(2)
    )
    other = got_ref[:width, :]
    kv0 = kv0 + jnp.where(is_second, other, 0.0)
    back1 = back1 + jnp.where(is_second, 0.0, other)
    chunks = half_rows // CHUNK
    kv_used, back_used = [kv0], [back1]
    for c in range(chunks - 1):
        kv_used.append(kv_used[-1] + keep_ref[0, c])
        back_used.insert(0, back_used[0] + keep_ref[1, chunks - 1 - c])
    kv_used = [state.astype(BF16) for state in kv_used]
    back_used = [state.astype(BF16) for state in back_used]
    copies = []

    def put(i, values, rows):
        for c, value in values:
            buffers[i][pl.ds(c * CHUNK, CHUNK), :] = value.astype(BF16)
        copy = pltpu.make_async_copy(
            buffers[i].at[rows, :], outs[i].at[rows, :], sems.at[len(copies)]
        )
        copy.start()
        copies.append(copy)

    def at(ref, c):
        return ref[pl.ds(c * CHUNK, CHUNK), :]

    att, qg, kg, vg = local
    for b in range(2):
        part = range(b * chunks // 2, (b + 1) * chunks // 2)
        rows = pl.ds(b * half_rows // 2, half_rows // 2)
        put(1, [(c, at(qg, c) + dot(at(g_ref, c), kv_used[c], 1, 1)) for c in part], rows)
        put(2, [(c, at(kg, c) + dot(at(v_ref, c), back_used[c], 1, 1)) for c in part], rows)
        put(3, [(c, at(vg, c) + dot(at(k_ref, c), back_used[c], 1, 0)) for c in part], rows)
        put(
            0,
            [
                (c, (at(att, c) + dot(at(q_ref, c), kv_used[c], 1, 0)) * at(scale_ref, c))
                for c in part
            ],
            rows,
        )
    for copy in copies:
        copy.wait()


def in_memory(array):
    return pltpu.with_memory_space_constraint(array, pltpu.HBM)


def call(kernel, outs, limit, **options):
    return pl.pallas_call(
        kernel,
        out_shape=outs,
        compiler_params=pltpu.CompilerParams(vmem_limit_bytes=limit),
        **options,
    )


def per_device(pairs, groups, queries, key_vectors, value_vectors, out_grad):
    half_rows, width = queries.shape
    rows16 = jax.ShapeDtypeStruct((half_rows, width), BF16)
    rows32 = jax.ShapeDtypeStruct((half_rows, width), F32)
    states = jax.ShapeDtypeStruct((2, half_rows // CHUNK, width, width), F32)
    half = width // 2
    halves = jax.ShapeDtypeStruct((2, half, width), F32)
    sent = jax.ShapeDtypeStruct((width + half, width), F32)
    in_hbm = pl.BlockSpec(memory_space=pltpu.HBM)
    in_vmem = pl.BlockSpec(memory_space=pltpu.VMEM)
    anywhere = pl.BlockSpec(memory_space=pl.ANY)
    send, own, keep, q, k, v, grad, scale = call(
        outer_kernel,
        (sent, halves, states) + (rows16,) * 4 + (rows32,),
        2**23,
        in_specs=[in_hbm] * 4,
        scratch_shapes=[
            pltpu.VMEM((half_rows, width), BF16),
            pltpu.VMEM((2, width, width), F32),
            pltpu.SemaphoreType.DMA((4,)),
        ],
    )(*(in_memory(x) for x in (queries, key_vectors, value_vectors, out_grad)))

    got = lax.ppermute(send, AXES, pairs)
    local = call(
        local_kernel,
        (rows32,) * 4,
        2**24,
        cost_estimate=pl.CostEstimate(
            flops=12 * half_rows * CHUNK * width, bytes_accessed=2**22, transcendentals=0
        ),
    )(q, k, v, grad)
    count = lax.axis_size("seq")
    quarter = half // 2
    parts = call(
        spread_kernel,
        jax.ShapeDtypeStruct((count, quarter, width), F32),
        2**23,
        in_specs=[in_vmem] * 2 + [anywhere],
    )(own, got, local[0])
    parts = lax.all_to_all(parts, "seq", 0, 0)
    quads = jax.ShapeDtypeStruct((4, 2, quarter, width), F32)
    state = call(gather_kernel, quads, 2**23)(parts)
    state = lax.all_to_all(state, AXES, 0, 0, axis_index_groups=groups)
    return call(
        final_kernel,
        (rows16,) * 4,
        2**24,
        out_specs=(in_hbm,) * 4,
        scratch_shapes=[pltpu.VMEM((half_rows, width), BF16)] * 4
        + [pltpu.SemaphoreType.DMA((8,))],
    )(q, k, v, grad, scale, state, got, keep, *local)


def solution(mesh):
    n_seq, n_inner = mesh.shape["seq"], mesh.shape["inner"]
    pairs = [(i, i ^ 1) for i in range(n_seq * n_inner)]
    groups = [
        [(2 * x + z) * n_inner + 2 * h + side for z in range(2) for side in range(2)]
        for x in range(n_seq // 2)
        for h in range(n_inner // 2)
    ]
    spec = P("seq", "inner")
    return jax.shard_map(
        functools.partial(per_device, pairs, groups),
        mesh=mesh,
        in_specs=(spec,) * 4,
        out_specs=(spec,) * 4,
        check_vma=False,
    )
```

```python
import functools

import jax
import jax.numpy as jnp
from jax import lax
from jax.experimental import pallas as pl
from jax.experimental.pallas import tpu as pltpu
from jax.sharding import PartitionSpec as P

BLOCK = 512
SUB = 256
AXES = ("seq", "inner")
F32 = jnp.float32
BF16 = jnp.bfloat16


def dot(a, b, ca, cb):
    return lax.dot_general(a, b, (((ca,), (cb,)), ((), ())), preferred_element_type=F32)


def scaling_of(start, rows, width):
    row = lax.broadcasted_iota(jnp.int32, (rows, width), 0)
    position = (start + row).astype(F32)
    return lax.rsqrt(width * (position + 1.0))


def first_position(half_rows):
    return (lax.axis_index("seq") * 2 + lax.axis_index("inner") % 2) * half_rows


def outer_kernel(
    q_hbm, k_hbm, v_hbm, o_hbm,
    send_ref, own_ref, keep_ref, q_ref, k_ref, v_ref, grad_ref, scale_ref,
    o_ref, total_ref, sems,
):
    half_rows, width = q_ref.shape
    start = first_position(half_rows)
    pairs = ((k_hbm, k_ref), (v_hbm, v_ref), (o_hbm, o_ref), (q_hbm, q_ref))
    copies = [
        pltpu.make_async_copy(source, target, sems.at[i])
        for i, (source, target) in enumerate(pairs)
    ]
    for copy in copies:
        copy.start()
    scale_ref[...] = scaling_of(start, half_rows, width)
    for copy in copies:
        copy.wait()
    kv, back = [], []
    for b in range(half_rows // BLOCK):
        rows = pl.ds(b * BLOCK, BLOCK)
        grad = (scale_ref[rows, :] * o_ref[rows, :].astype(F32)).astype(BF16)
        grad_ref[rows, :] = grad
        kv.append(dot(k_ref[rows, :], v_ref[rows, :], 0, 0))
        back.append(dot(q_ref[rows, :], grad, 0, 0))
    keep_ref[:width, :] = kv[0]
    keep_ref[width:, :] = back[1]
    half = width // 2
    side = lax.axis_index("inner") % 2
    total_ref[0] = kv[0] + kv[1]
    total_ref[1] = back[0] + back[1]
    own_ref[0] = total_ref[0, pl.ds(side * half, half), :]
    own_ref[1] = total_ref[1, pl.ds(side * half, half), :]
    send_ref[:width, :] = total_ref[side]
    send_ref[width:, :] = total_ref[1 - side, pl.ds((1 - side) * half, half), :]


def spread_kernel(own_ref, got_ref, *refs):
    out_ref = refs[-1]
    count, rows, width = out_ref.shape
    half = width // 2
    me = lax.axis_index("seq")
    side = lax.axis_index("inner") % 2
    whole = got_ref[pl.ds(side * half, half), :]
    part = got_ref[width:, :]
    kv = own_ref[0] + jnp.where(side == 0, part, whole)
    back = own_ref[1] + jnp.where(side == 0, whole, part)
    for i in range(count):
        takes_kv = jnp.logical_or(i // 2 > me // 2, (i // 2 == me // 2) & (me % 2 == 0))
        cut = slice((i % 2) * rows, (i % 2 + 1) * rows)
        out_ref[i] = jnp.where(takes_kv, kv[cut], back[cut])


def gather_kernel(parts_ref, send_ref, mine_ref):
    pair = lax.axis_index("seq") // 2
    zero = jnp.zeros(parts_ref.shape[1:], F32)
    earlier, later = zero, zero
    count = parts_ref.shape[0]
    for i in range(count):
        earlier = earlier + jnp.where(i // 2 < pair, parts_ref[i], zero)
        j = count - 1 - i
        later = later + jnp.where(j // 2 > pair, parts_ref[j], zero)
    is_first = lax.axis_index("seq") % 2 == 0
    with_first = earlier + parts_ref[2 * pair]
    with_second = later + parts_ref[2 * pair + 1]
    mine_ref[0] = jnp.where(is_first, earlier, with_first)
    mine_ref[1] = jnp.where(is_first, with_second, later)
    send_ref[0] = jnp.where(is_first, with_first, earlier)
    send_ref[1] = jnp.where(is_first, later, with_second)


def join_kernel(mine_ref, got_ref, out_ref):
    rows = mine_ref.shape[1]
    place = lax.axis_index("seq") % 2
    for i in range(2):
        out_ref[i, pl.ds(place * rows, rows), :] = mine_ref[i]
        out_ref[i, pl.ds((1 - place) * rows, rows), :] = got_ref[i]


def local_kernel(q_ref, k_ref, v_ref, g_ref, after_ref, att_ref, qg_ref, kg_ref, vg_ref):
    row = lax.broadcasted_iota(jnp.int32, (SUB, SUB), 0)
    col = lax.broadcasted_iota(jnp.int32, (SUB, SUB), 1)
    causal = row >= col
    n = BLOCK // SUB

    def masked(scores):
        left = scores.shape[1] - SUB
        last = jnp.where(causal, scores[:, left:], 0.0)
        if left:
            last = jnp.concatenate([scores[:, :left], last], 1)
        return last.astype(BF16)

    for b in range(q_ref.shape[0] // BLOCK):
        weights, scores = [], []
        for i in range(n):
            own = pl.ds(b * BLOCK + i * SUB, SUB)
            before = pl.ds(b * BLOCK, (i + 1) * SUB)
            weights.append(masked(dot(q_ref[own, :], k_ref[before, :], 1, 1)))
            scores.append(masked(dot(g_ref[own, :], v_ref[before, :], 1, 1)))
            att_ref[own, :] = dot(weights[i], v_ref[before, :], 1, 0)
            qg_ref[own, :] = dot(scores[i], k_ref[before, :], 1, 0)
        for j in range(n):
            own = pl.ds(b * BLOCK + j * SUB, SUB)
            after = pl.ds(b * BLOCK + j * SUB, (n - j) * SUB)
            cut = slice(j * SUB, (j + 1) * SUB)
            w = jnp.concatenate([weights[i][:, cut] for i in range(j, n)], 0)
            s = jnp.concatenate([scores[i][:, cut] for i in range(j, n)], 0)
            vg_ref[own, :] = dot(w, g_ref[after, :], 0, 0)
            kg_ref[own, :] = dot(s, q_ref[after, :], 0, 0)


def final_kernel(
    q_ref, k_ref, v_ref, g_ref, scale_ref, mine_ref, theirs_ref, got_ref, keep_ref, *refs
):
    local, outs = refs[:4], refs[4:8]
    buffers, sems = refs[8:12], refs[12]
    half_rows, width = q_ref.shape
    is_second = lax.axis_index("inner") % 2 == 1
    kv0, back1 = (
        jnp.concatenate(
            [
                jnp.where(is_second, theirs_ref[i], mine_ref[i]),
                jnp.where(is_second, mine_ref[i], theirs_ref[i]),
            ],
            0,
        )
        for i in range(2)
    )
    other = got_ref[:width, :]
    kv0 = kv0 + jnp.where(is_second, other, 0.0)
    back1 = back1 + jnp.where(is_second, 0.0, other)
    kv_used = [kv0.astype(BF16), (kv0 + keep_ref[:width, :]).astype(BF16)]
    back_used = [(back1 + keep_ref[width:, :]).astype(BF16), back1.astype(BF16)]
    copies = []

    def put(i, value, rows):
        buffers[i][rows, :] = value.astype(BF16)
        copy = pltpu.make_async_copy(
            buffers[i].at[rows, :], outs[i].at[rows, :], sems.at[len(copies)]
        )
        copy.start()
        copies.append(copy)

    for b in range(half_rows // BLOCK):
        rows = pl.ds(b * BLOCK, BLOCK)
        q, k, v, g = q_ref[rows, :], k_ref[rows, :], v_ref[rows, :], g_ref[rows, :]
        att, qg, kg, vg = (ref[rows, :] for ref in local)
        put(1, qg + dot(g, kv_used[b], 1, 1), rows)
        put(2, kg + dot(v, back_used[b], 1, 1), rows)
        put(3, vg + dot(k, back_used[b], 1, 0), rows)
        put(0, (att + dot(q, kv_used[b], 1, 0)) * scale_ref[rows, :], rows)
    for copy in copies:
        copy.wait()


def in_memory(array):
    return pltpu.with_memory_space_constraint(array, pltpu.HBM)


def call(kernel, outs, limit, **options):
    return pl.pallas_call(
        kernel,
        out_shape=outs,
        compiler_params=pltpu.CompilerParams(vmem_limit_bytes=limit),
        **options,
    )


def per_device(sides, neighbours, queries, key_vectors, value_vectors, out_grad):
    half_rows, width = queries.shape
    blocks = half_rows // BLOCK
    rows16 = jax.ShapeDtypeStruct((half_rows, width), BF16)
    rows32 = jax.ShapeDtypeStruct((half_rows, width), F32)
    states = jax.ShapeDtypeStruct((2 * width, width), F32)
    half = width // 2
    halves = jax.ShapeDtypeStruct((2, half, width), F32)
    sent = jax.ShapeDtypeStruct((width + half, width), F32)
    in_hbm = pl.BlockSpec(memory_space=pltpu.HBM)
    in_vmem = pl.BlockSpec(memory_space=pltpu.VMEM)
    anywhere = pl.BlockSpec(memory_space=pl.ANY)
    send, own, keep, q, k, v, grad, scale = call(
        outer_kernel,
        (sent, halves, states) + (rows16,) * 4 + (rows32,),
        2**23,
        in_specs=[in_hbm] * 4,
        scratch_shapes=[
            pltpu.VMEM((half_rows, width), BF16),
            pltpu.VMEM((2, width, width), F32),
            pltpu.SemaphoreType.DMA((4,)),
        ],
    )(*(in_memory(x) for x in (queries, key_vectors, value_vectors, out_grad)))

    got = lax.ppermute(send, AXES, sides)
    count = lax.axis_size("seq")
    quarter = half // 2
    parts = call(
        spread_kernel, jax.ShapeDtypeStruct((count, quarter, width), F32), 2**23
    )(own, got)
    parts = lax.all_to_all(parts, "seq", 0, 0)
    quarters = jax.ShapeDtypeStruct((2, quarter, width), F32)
    send, mine = call(gather_kernel, (quarters,) * 2, 2**23)(parts)
    near = lax.ppermute(send, AXES, neighbours)
    local = call(
        local_kernel,
        (rows32,) * 4,
        2**24,
        in_specs=[in_vmem] * 4 + [anywhere],
        cost_estimate=pl.CostEstimate(
            flops=12 * half_rows * BLOCK * width, bytes_accessed=2**22, transcendentals=0
        ),
    )(q, k, v, grad, mine)
    mine = call(join_kernel, halves, 2**23)(mine, near)
    theirs = lax.ppermute(mine, AXES, sides)
    return call(
        final_kernel,
        (rows16,) * 4,
        2**24,
        out_specs=(in_hbm,) * 4,
        scratch_shapes=[pltpu.VMEM((half_rows, width), BF16)] * 4
        + [pltpu.SemaphoreType.DMA((4 * blocks,))],
    )(q, k, v, grad, scale, mine, theirs, got, keep, *local)


def solution(mesh):
    n_seq, n_inner = mesh.shape["seq"], mesh.shape["inner"]
    sides = [(i, i ^ 1) for i in range(n_seq * n_inner)]
    neighbours = [
        (s * n_inner + i, (s ^ 1) * n_inner + i) for s in range(n_seq) for i in range(n_inner)
    ]
    spec = P("seq", "inner")
    return jax.shard_map(
        functools.partial(per_device, sides, neighbours),
        mesh=mesh,
        in_specs=(spec,) * 4,
        out_specs=(spec,) * 4,
        check_vma=False,
    )
```

```python
import functools

import jax
import jax.numpy as jnp
from jax import lax
from jax.experimental import pallas as pl
from jax.experimental.pallas import tpu as pltpu
from jax.sharding import PartitionSpec as P

BLOCK = 512
SUB = 256
AXES = ("seq", "inner")
F32 = jnp.float32
BF16 = jnp.bfloat16


def dot(a, b, ca, cb):
    return lax.dot_general(a, b, (((ca,), (cb,)), ((), ())), preferred_element_type=F32)


def scaling_of(start, rows, width):
    row = lax.broadcasted_iota(jnp.int32, (rows, width), 0)
    position = (start + row).astype(F32)
    return lax.rsqrt(width * (position + 1.0))


def first_position(half_rows):
    return (lax.axis_index("seq") * 2 + lax.axis_index("inner") % 2) * half_rows


def waits_at_start():
    place = lax.axis_index("inner")
    near = (place > 0) & (place < lax.axis_size("inner") // 4)
    return (lax.axis_index("seq") == 0) & near


def in_block(q_ref, k_ref, v_ref, g_ref, outs):
    att_ref, qg_ref, kg_ref, vg_ref = outs
    row = lax.broadcasted_iota(jnp.int32, (SUB, SUB), 0)
    col = lax.broadcasted_iota(jnp.int32, (SUB, SUB), 1)
    causal = row >= col
    n = BLOCK // SUB
    blocks = range(q_ref.shape[0] // BLOCK)

    def tiles(b, first, count):
        return pl.ds(b * BLOCK + first * SUB, count * SUB)

    def masked(scores):
        left = scores.shape[1] - SUB
        last = jnp.where(causal, scores[:, left:], 0.0)
        if left:
            last = jnp.concatenate([scores[:, :left], last], 1)
        return last.astype(BF16)

    weights, scores = {}, {}
    for b in blocks:
        for i in range(n):
            own, before = tiles(b, i, 1), tiles(b, 0, i + 1)
            weights[b, i] = masked(dot(q_ref[own, :], k_ref[before, :], 1, 1))
            scores[b, i] = masked(dot(g_ref[own, :], v_ref[before, :], 1, 1))
    for b in blocks:
        for i in range(n):
            own, before = tiles(b, i, 1), tiles(b, 0, i + 1)
            att_ref[own, :] = dot(weights[b, i], v_ref[before, :], 1, 0)
            qg_ref[own, :] = dot(scores[b, i], k_ref[before, :], 1, 0)
    for b in blocks:
        for j in range(n):
            own, after = tiles(b, j, 1), tiles(b, j, n - j)
            cut = slice(j * SUB, (j + 1) * SUB)
            w = jnp.concatenate([weights[b, i][:, cut] for i in range(j, n)], 0)
            s = jnp.concatenate([scores[b, i][:, cut] for i in range(j, n)], 0)
            vg_ref[own, :] = dot(w, g_ref[after, :], 0, 0)
            kg_ref[own, :] = dot(s, q_ref[after, :], 0, 0)


def outer_kernel(
    q_hbm, k_hbm, v_hbm, o_hbm,
    send_ref, own_ref, keep_ref, q_ref, k_ref, v_ref, grad_ref, scale_ref,
    att_ref, qg_ref, kg_ref, vg_ref,
    o_ref, total_ref, sems,
):
    half_rows, width = q_ref.shape
    start = first_position(half_rows)
    pairs = ((k_hbm, k_ref), (v_hbm, v_ref), (o_hbm, o_ref), (q_hbm, q_ref))
    copies = [
        pltpu.make_async_copy(source, target, sems.at[i])
        for i, (source, target) in enumerate(pairs)
    ]
    for copy in copies:
        copy.start()
    scale_ref[...] = scaling_of(start, half_rows, width)
    for copy in copies:
        copy.wait()
    kv, back = [], []
    for b in range(half_rows // BLOCK):
        rows = pl.ds(b * BLOCK, BLOCK)
        grad = (scale_ref[rows, :] * o_ref[rows, :].astype(F32)).astype(BF16)
        grad_ref[rows, :] = grad
        kv.append(dot(k_ref[rows, :], v_ref[rows, :], 0, 0))
        back.append(dot(q_ref[rows, :], grad, 0, 0))
    keep_ref[:width, :] = kv[0]
    keep_ref[width:, :] = back[1]
    half = width // 2
    side = lax.axis_index("inner") % 2
    total_ref[0] = kv[0] + kv[1]
    total_ref[1] = back[0] + back[1]
    own_ref[0] = total_ref[0, pl.ds(side * half, half), :]
    own_ref[1] = total_ref[1, pl.ds(side * half, half), :]
    send_ref[:width, :] = total_ref[side]
    send_ref[width:, :] = total_ref[1 - side, pl.ds((1 - side) * half, half), :]

    @pl.when(waits_at_start())
    def _():
        in_block(q_ref, k_ref, v_ref, grad_ref, (att_ref, qg_ref, kg_ref, vg_ref))


def spread_kernel(own_ref, got_ref, out_ref):
    count, rows, width = out_ref.shape
    half = width // 2
    me = lax.axis_index("seq")
    side = lax.axis_index("inner") % 2
    whole = got_ref[pl.ds(side * half, half), :]
    part = got_ref[width:, :]
    kv = own_ref[0] + jnp.where(side == 0, part, whole)
    back = own_ref[1] + jnp.where(side == 0, whole, part)
    for i in range(count):
        takes_kv = jnp.logical_or(i // 2 > me // 2, (i // 2 == me // 2) & (me % 2 == 0))
        cut = slice((i % 2) * rows, (i % 2 + 1) * rows)
        out_ref[i] = jnp.where(takes_kv, kv[cut], back[cut])


def gather_kernel(parts_ref, send_ref):
    pair = lax.axis_index("seq") // 2
    zero = jnp.zeros(parts_ref.shape[1:], F32)
    earlier, later = zero, zero
    count = parts_ref.shape[0]
    for i in range(count):
        earlier = earlier + jnp.where(i // 2 < pair, parts_ref[i], zero)
        j = count - 1 - i
        later = later + jnp.where(j // 2 > pair, parts_ref[j], zero)
    with_first = earlier + parts_ref[2 * pair]
    with_second = later + parts_ref[2 * pair + 1]
    for side in range(2):
        send_ref[side, 0] = earlier
        send_ref[side, 1] = with_second
        send_ref[2 + side, 0] = with_first
        send_ref[2 + side, 1] = later


def final_kernel(
    q_ref, k_ref, v_ref, g_ref, scale_ref, state_ref, got_ref, keep_ref, *refs
):
    local, outs = refs[:4], refs[4:8]
    buffers, here, sems = refs[8:12], refs[12:16], refs[16]
    half_rows, width = q_ref.shape
    is_second = lax.axis_index("inner") % 2 == 1
    kv0, back1 = (
        jnp.concatenate([state_ref[2 * z + c, i] for c in range(2) for z in range(2)], 0)
        for i in range(2)
    )
    other = got_ref[:width, :]
    kv0 = kv0 + jnp.where(is_second, other, 0.0)
    back1 = back1 + jnp.where(is_second, 0.0, other)
    kv_used = [kv0.astype(BF16), (kv0 + keep_ref[:width, :]).astype(BF16)]
    back_used = [(back1 + keep_ref[width:, :]).astype(BF16), back1.astype(BF16)]

    def finish(local):
        copies = []

        def put(i, value, rows):
            buffers[i][rows, :] = value.astype(BF16)
            copy = pltpu.make_async_copy(
                buffers[i].at[rows, :], outs[i].at[rows, :], sems.at[len(copies)]
            )
            copy.start()
            copies.append(copy)

        for b in range(half_rows // BLOCK):
            rows = pl.ds(b * BLOCK, BLOCK)
            q, k, v, g = q_ref[rows, :], k_ref[rows, :], v_ref[rows, :], g_ref[rows, :]
            att, qg, kg, vg = (ref[rows, :] for ref in local)
            put(1, qg + dot(g, kv_used[b], 1, 1), rows)
            put(2, kg + dot(v, back_used[b], 1, 1), rows)
            put(3, vg + dot(k, back_used[b], 1, 0), rows)
            put(0, (att + dot(q, kv_used[b], 1, 0)) * scale_ref[rows, :], rows)
        for copy in copies:
            copy.wait()

    ready = waits_at_start()

    @pl.when(ready)
    def _():
        finish(local)

    @pl.when(jnp.logical_not(ready))
    def _():
        in_block(q_ref, k_ref, v_ref, g_ref, here)
        finish(here)


def in_memory(array):
    return pltpu.with_memory_space_constraint(array, pltpu.HBM)


def call(kernel, outs, limit, **options):
    return pl.pallas_call(
        kernel,
        out_shape=outs,
        compiler_params=pltpu.CompilerParams(vmem_limit_bytes=limit),
        **options,
    )


def per_device(pairs, groups, queries, key_vectors, value_vectors, out_grad):
    half_rows, width = queries.shape
    blocks = half_rows // BLOCK
    rows16 = jax.ShapeDtypeStruct((half_rows, width), BF16)
    rows32 = jax.ShapeDtypeStruct((half_rows, width), F32)
    states = jax.ShapeDtypeStruct((2 * width, width), F32)
    half = width // 2
    halves = jax.ShapeDtypeStruct((2, half, width), F32)
    sent = jax.ShapeDtypeStruct((width + half, width), F32)
    in_hbm = pl.BlockSpec(memory_space=pltpu.HBM)
    send, own, keep, q, k, v, grad, scale, *local = call(
        outer_kernel,
        (sent, halves, states) + (rows16,) * 4 + (rows32,) * 5,
        2**24,
        in_specs=[in_hbm] * 4,
        scratch_shapes=[
            pltpu.VMEM((half_rows, width), BF16),
            pltpu.VMEM((2, width, width), F32),
            pltpu.SemaphoreType.DMA((4,)),
        ],
    )(*(in_memory(x) for x in (queries, key_vectors, value_vectors, out_grad)))

    got = lax.ppermute(send, AXES, pairs)
    count = lax.axis_size("seq")
    quarter = half // 2
    parts = call(
        spread_kernel,
        jax.ShapeDtypeStruct((count, quarter, width), F32),
        2**23,
    )(own, got)
    parts = lax.all_to_all(parts, "seq", 0, 0)
    quads = jax.ShapeDtypeStruct((4, 2, quarter, width), F32)
    state = call(gather_kernel, quads, 2**23)(parts)
    state = lax.all_to_all(state, AXES, 0, 0, axis_index_groups=groups)
    return call(
        final_kernel,
        (rows16,) * 4,
        2**24,
        out_specs=(in_hbm,) * 4,
        scratch_shapes=[pltpu.VMEM((half_rows, width), BF16)] * 4
        + [pltpu.VMEM((half_rows, width), F32)] * 4
        + [pltpu.SemaphoreType.DMA((4 * blocks,))],
    )(q, k, v, grad, scale, state, got, keep, *local)


def solution(mesh):
    n_seq, n_inner = mesh.shape["seq"], mesh.shape["inner"]
    pairs = [(i, i ^ 1) for i in range(n_seq * n_inner)]
    groups = [
        [(2 * x + z) * n_inner + 2 * h + side for z in range(2) for side in range(2)]
        for x in range(n_seq // 2)
        for h in range(n_inner // 2)
    ]
    spec = P("seq", "inner")
    return jax.shard_map(
        functools.partial(per_device, pairs, groups),
        mesh=mesh,
        in_specs=(spec,) * 4,
        out_specs=(spec,) * 4,
        check_vma=False,
    )
```

```python
import functools

import jax
import jax.numpy as jnp
from jax import lax
from jax.experimental import pallas as pl
from jax.experimental.pallas import tpu as pltpu
from jax.sharding import PartitionSpec as P

BLOCK = 512
SUB = 256
AXES = ("seq", "inner")
F32 = jnp.float32
BF16 = jnp.bfloat16


def dot(a, b, ca, cb):
    return lax.dot_general(a, b, (((ca,), (cb,)), ((), ())), preferred_element_type=F32)


def scaling_of(start, rows, width):
    row = lax.broadcasted_iota(jnp.int32, (rows, width), 0)
    position = (start + row).astype(F32)
    return lax.rsqrt(width * (position + 1.0))


def first_position(half_rows):
    return (lax.axis_index("seq") * 2 + lax.axis_index("inner") % 2) * half_rows


def waits_at_start():
    place = lax.axis_index("inner")
    near = (place > 0) & (place < lax.axis_size("inner") // 4)
    return (lax.axis_index("seq") == 0) & near


def in_block(q_ref, k_ref, v_ref, g_ref, outs):
    att_ref, qg_ref, kg_ref, vg_ref = outs
    row = lax.broadcasted_iota(jnp.int32, (SUB, SUB), 0)
    col = lax.broadcasted_iota(jnp.int32, (SUB, SUB), 1)
    causal = row >= col
    n = BLOCK // SUB
    blocks = range(q_ref.shape[0] // BLOCK)

    def tiles(b, first, count):
        return pl.ds(b * BLOCK + first * SUB, count * SUB)

    def masked(scores):
        left = scores.shape[1] - SUB
        last = jnp.where(causal, scores[:, left:], 0.0)
        if left:
            last = jnp.concatenate([scores[:, :left], last], 1)
        return last.astype(BF16)

    weights, scores = {}, {}
    for b in blocks:
        for i in range(n):
            own, before = tiles(b, i, 1), tiles(b, 0, i + 1)
            weights[b, i] = masked(dot(q_ref[own, :], k_ref[before, :], 1, 1))
            scores[b, i] = masked(dot(g_ref[own, :], v_ref[before, :], 1, 1))
    for b in blocks:
        for i in range(n):
            own, before = tiles(b, i, 1), tiles(b, 0, i + 1)
            att_ref[own, :] = dot(weights[b, i], v_ref[before, :], 1, 0)
            qg_ref[own, :] = dot(scores[b, i], k_ref[before, :], 1, 0)
    for b in blocks:
        for j in range(n):
            own, after = tiles(b, j, 1), tiles(b, j, n - j)
            cut = slice(j * SUB, (j + 1) * SUB)
            w = jnp.concatenate([weights[b, i][:, cut] for i in range(j, n)], 0)
            s = jnp.concatenate([scores[b, i][:, cut] for i in range(j, n)], 0)
            vg_ref[own, :] = dot(w, g_ref[after, :], 0, 0)
            kg_ref[own, :] = dot(s, q_ref[after, :], 0, 0)


def outer_kernel(
    q_hbm, k_hbm, v_hbm, o_hbm,
    send_ref, own_ref, keep_ref, q_ref, k_ref, v_ref, grad_ref, scale_ref,
    att_ref, qg_ref, kg_ref, vg_ref,
    o_ref, total_ref, sems,
):
    half_rows, width = q_ref.shape
    start = first_position(half_rows)
    pairs = ((k_hbm, k_ref), (v_hbm, v_ref), (o_hbm, o_ref), (q_hbm, q_ref))
    copies = [
        pltpu.make_async_copy(source, target, sems.at[i])
        for i, (source, target) in enumerate(pairs)
    ]
    for copy in copies:
        copy.start()
    scale_ref[...] = scaling_of(start, half_rows, width)
    for copy in copies:
        copy.wait()
    kv, back = [], []
    for b in range(half_rows // BLOCK):
        rows = pl.ds(b * BLOCK, BLOCK)
        grad = (scale_ref[rows, :] * o_ref[rows, :].astype(F32)).astype(BF16)
        grad_ref[rows, :] = grad
        kv.append(dot(k_ref[rows, :], v_ref[rows, :], 0, 0))
        back.append(dot(q_ref[rows, :], grad, 0, 0))
    keep_ref[:width, :] = kv[0]
    keep_ref[width:, :] = back[1]
    half = width // 2
    side = lax.axis_index("inner") % 2
    total_ref[0] = kv[0] + kv[1]
    total_ref[1] = back[0] + back[1]
    own_ref[0] = total_ref[0, pl.ds(side * half, half), :]
    own_ref[1] = total_ref[1, pl.ds(side * half, half), :]
    send_ref[:width, :] = total_ref[side]
    send_ref[width:, :] = total_ref[1 - side, pl.ds((1 - side) * half, half), :]

    @pl.when(waits_at_start())
    def _():
        in_block(q_ref, k_ref, v_ref, grad_ref, (att_ref, qg_ref, kg_ref, vg_ref))


def spread_kernel(own_ref, got_ref, out_ref):
    count, rows, width = out_ref.shape
    half = width // 2
    me = lax.axis_index("seq")
    side = lax.axis_index("inner") % 2
    whole = got_ref[pl.ds(side * half, half), :]
    part = got_ref[width:, :]
    kv = own_ref[0] + jnp.where(side == 0, part, whole)
    back = own_ref[1] + jnp.where(side == 0, whole, part)
    pairs = count // 2
    for z in range(2):
        cut = slice(z * rows, (z + 1) * rows)
        for x in range(pairs):
            takes_kv = jnp.logical_or(x > me // 2, (x == me // 2) & (me % 2 == 0))
            out_ref[z * pairs + x] = jnp.where(takes_kv, kv[cut], back[cut])


def gather_kernel(parts_ref, send_ref):
    pair = lax.axis_index("seq") // 2
    zero = jnp.zeros(parts_ref.shape[1:], F32)
    earlier, later = zero, zero
    pairs = parts_ref.shape[0] // 2
    for x in range(pairs):
        y = pairs - 1 - x
        for z in range(2):
            earlier = earlier + jnp.where(x < pair, parts_ref[z * pairs + x], zero)
            later = later + jnp.where(y > pair, parts_ref[z * pairs + y], zero)
    with_first = earlier + parts_ref[pair]
    with_second = later + parts_ref[pairs + pair]
    for side in range(2):
        send_ref[side, 0] = earlier
        send_ref[side, 1] = with_second
        send_ref[2 + side, 0] = with_first
        send_ref[2 + side, 1] = later


def final_kernel(
    q_ref, k_ref, v_ref, g_ref, scale_ref, state_ref, got_ref, keep_ref, *refs
):
    local, outs = refs[:4], refs[4:8]
    buffers, here, sems = refs[8:12], refs[12:16], refs[16]
    half_rows, width = q_ref.shape
    is_second = lax.axis_index("inner") % 2 == 1
    kv0, back1 = (
        jnp.concatenate([state_ref[2 * z + c, i] for c in range(2) for z in range(2)], 0)
        for i in range(2)
    )
    other = got_ref[:width, :]
    kv0 = kv0 + jnp.where(is_second, other, 0.0)
    back1 = back1 + jnp.where(is_second, 0.0, other)
    kv_used = [kv0.astype(BF16), (kv0 + keep_ref[:width, :]).astype(BF16)]
    back_used = [(back1 + keep_ref[width:, :]).astype(BF16), back1.astype(BF16)]

    def finish(local):
        copies = []

        def put(i, value, rows):
            buffers[i][rows, :] = value.astype(BF16)
            copy = pltpu.make_async_copy(
                buffers[i].at[rows, :], outs[i].at[rows, :], sems.at[len(copies)]
            )
            copy.start()
            copies.append(copy)

        for b in range(half_rows // BLOCK):
            rows = pl.ds(b * BLOCK, BLOCK)
            q, k, v, g = q_ref[rows, :], k_ref[rows, :], v_ref[rows, :], g_ref[rows, :]
            att, qg, kg, vg = (ref[rows, :] for ref in local)
            put(1, qg + dot(g, kv_used[b], 1, 1), rows)
            put(2, kg + dot(v, back_used[b], 1, 1), rows)
            put(3, vg + dot(k, back_used[b], 1, 0), rows)
            put(0, (att + dot(q, kv_used[b], 1, 0)) * scale_ref[rows, :], rows)
        for copy in copies:
            copy.wait()

    ready = waits_at_start()

    @pl.when(ready)
    def _():
        finish(local)

    @pl.when(jnp.logical_not(ready))
    def _():
        in_block(q_ref, k_ref, v_ref, g_ref, here)
        finish(here)


def in_memory(array):
    return pltpu.with_memory_space_constraint(array, pltpu.HBM)


def call(kernel, outs, limit, **options):
    return pl.pallas_call(
        kernel,
        out_shape=outs,
        compiler_params=pltpu.CompilerParams(vmem_limit_bytes=limit),
        **options,
    )


def per_device(pairs, lines, groups, queries, key_vectors, value_vectors, out_grad):
    half_rows, width = queries.shape
    blocks = half_rows // BLOCK
    rows16 = jax.ShapeDtypeStruct((half_rows, width), BF16)
    rows32 = jax.ShapeDtypeStruct((half_rows, width), F32)
    states = jax.ShapeDtypeStruct((2 * width, width), F32)
    half = width // 2
    halves = jax.ShapeDtypeStruct((2, half, width), F32)
    sent = jax.ShapeDtypeStruct((width + half, width), F32)
    in_hbm = pl.BlockSpec(memory_space=pltpu.HBM)
    send, own, keep, q, k, v, grad, scale, *local = call(
        outer_kernel,
        (sent, halves, states) + (rows16,) * 4 + (rows32,) * 5,
        2**24,
        in_specs=[in_hbm] * 4,
        scratch_shapes=[
            pltpu.VMEM((half_rows, width), BF16),
            pltpu.VMEM((2, width, width), F32),
            pltpu.SemaphoreType.DMA((4,)),
        ],
    )(*(in_memory(x) for x in (queries, key_vectors, value_vectors, out_grad)))

    got = lax.ppermute(send, AXES, pairs)
    count = lax.axis_size("seq")
    quarter = half // 2
    parts = call(
        spread_kernel,
        jax.ShapeDtypeStruct((count, quarter, width), F32),
        2**23,
    )(own, got)
    parts = lax.all_to_all(parts, AXES, 0, 0, axis_index_groups=lines)
    quads = jax.ShapeDtypeStruct((4, 2, quarter, width), F32)
    state = call(gather_kernel, quads, 2**23)(parts)
    state = lax.all_to_all(state, AXES, 0, 0, axis_index_groups=groups)
    return call(
        final_kernel,
        (rows16,) * 4,
        2**24,
        out_specs=(in_hbm,) * 4,
        scratch_shapes=[pltpu.VMEM((half_rows, width), BF16)] * 4
        + [pltpu.VMEM((half_rows, width), F32)] * 4
        + [pltpu.SemaphoreType.DMA((4 * blocks,))],
    )(q, k, v, grad, scale, state, got, keep, *local)


def solution(mesh):
    n_seq, n_inner = mesh.shape["seq"], mesh.shape["inner"]
    pairs = [(i, i ^ 1) for i in range(n_seq * n_inner)]
    lines = [
        [(2 * x + z) * n_inner + i for z in range(2) for x in range(n_seq // 2)]
        for i in range(n_inner)
    ]
    groups = [
        [(2 * x + z) * n_inner + 2 * h + side for z in range(2) for side in range(2)]
        for x in range(n_seq // 2)
        for h in range(n_inner // 2)
    ]
    spec = P("seq", "inner")
    return jax.shard_map(
        functools.partial(per_device, pairs, lines, groups),
        mesh=mesh,
        in_specs=(spec,) * 4,
        out_specs=(spec,) * 4,
        check_vma=False,
    )
```

```python
import functools

import jax
import jax.numpy as jnp
from jax import lax
from jax.experimental import pallas as pl
from jax.experimental.pallas import tpu as pltpu
from jax.sharding import PartitionSpec as P

BLOCK = 512
SUB = 256
AXES = ("seq", "inner")
F32 = jnp.float32
BF16 = jnp.bfloat16


def dot(a, b, ca, cb):
    return lax.dot_general(a, b, (((ca,), (cb,)), ((), ())), preferred_element_type=F32)


def scaling_of(start, rows, width):
    row = lax.broadcasted_iota(jnp.int32, (rows, width), 0)
    position = (start + row).astype(F32)
    return lax.rsqrt(width * (position + 1.0))


def first_position(half_rows):
    return (lax.axis_index("seq") * 2 + lax.axis_index("inner") % 2) * half_rows


def waits_at_start():
    place = lax.axis_index("inner")
    near = (place > 0) & (place < lax.axis_size("inner") // 4)
    return (lax.axis_index("seq") == 0) & near


def in_block(q_ref, k_ref, v_ref, g_ref, outs):
    att_ref, qg_ref, kg_ref, vg_ref = outs
    row = lax.broadcasted_iota(jnp.int32, (SUB, SUB), 0)
    col = lax.broadcasted_iota(jnp.int32, (SUB, SUB), 1)
    causal = row >= col
    n = BLOCK // SUB
    blocks = range(q_ref.shape[0] // BLOCK)

    def tiles(b, first, count):
        return pl.ds(b * BLOCK + first * SUB, count * SUB)

    def masked(scores):
        left = scores.shape[1] - SUB
        last = jnp.where(causal, scores[:, left:], 0.0)
        if left:
            last = jnp.concatenate([scores[:, :left], last], 1)
        return last.astype(BF16)

    weights, scores = {}, {}
    for b in blocks:
        for i in range(n):
            own, before = tiles(b, i, 1), tiles(b, 0, i + 1)
            weights[b, i] = masked(dot(q_ref[own, :], k_ref[before, :], 1, 1))
            scores[b, i] = masked(dot(g_ref[own, :], v_ref[before, :], 1, 1))
    for b in blocks:
        for i in range(n):
            own, before = tiles(b, i, 1), tiles(b, 0, i + 1)
            att_ref[own, :] = dot(weights[b, i], v_ref[before, :], 1, 0)
            qg_ref[own, :] = dot(scores[b, i], k_ref[before, :], 1, 0)
    for b in blocks:
        for j in range(n):
            own, after = tiles(b, j, 1), tiles(b, j, n - j)
            cut = slice(j * SUB, (j + 1) * SUB)
            w = jnp.concatenate([weights[b, i][:, cut] for i in range(j, n)], 0)
            s = jnp.concatenate([scores[b, i][:, cut] for i in range(j, n)], 0)
            vg_ref[own, :] = dot(w, g_ref[after, :], 0, 0)
            kg_ref[own, :] = dot(s, q_ref[after, :], 0, 0)


def outer_kernel(
    q_hbm, k_hbm, v_hbm, o_hbm,
    send_ref, own_ref, keep_ref, q_ref, k_ref, v_ref, grad_ref, scale_ref,
    att_ref, qg_ref, kg_ref, vg_ref,
    o_ref, total_ref, sems,
):
    half_rows, width = q_ref.shape
    start = first_position(half_rows)
    pairs = ((k_hbm, k_ref), (v_hbm, v_ref), (o_hbm, o_ref), (q_hbm, q_ref))
    copies = [
        pltpu.make_async_copy(source, target, sems.at[i])
        for i, (source, target) in enumerate(pairs)
    ]
    for copy in copies:
        copy.start()
    scale_ref[...] = scaling_of(start, half_rows, width)
    for copy in copies:
        copy.wait()
    kv, back = [], []
    for b in range(half_rows // BLOCK):
        rows = pl.ds(b * BLOCK, BLOCK)
        grad = (scale_ref[rows, :] * o_ref[rows, :].astype(F32)).astype(BF16)
        grad_ref[rows, :] = grad
        kv.append(dot(k_ref[rows, :], v_ref[rows, :], 0, 0))
        back.append(dot(q_ref[rows, :], grad, 0, 0))
    keep_ref[:width, :] = kv[0]
    keep_ref[width:, :] = back[1]
    half = width // 2
    side = lax.axis_index("inner") % 2
    total_ref[0] = kv[0] + kv[1]
    total_ref[1] = back[0] + back[1]
    own_ref[0] = total_ref[0, pl.ds(side * half, half), :]
    own_ref[1] = total_ref[1, pl.ds(side * half, half), :]
    send_ref[:width, :] = total_ref[side]
    send_ref[width:, :] = total_ref[1 - side, pl.ds((1 - side) * half, half), :]

    @pl.when(waits_at_start())
    def _():
        in_block(q_ref, k_ref, v_ref, grad_ref, (att_ref, qg_ref, kg_ref, vg_ref))


def spread_kernel(own_ref, got_ref, out_ref):
    count, rows, width = out_ref.shape
    half = width // 2
    me = lax.axis_index("seq")
    side = lax.axis_index("inner") % 2
    whole = got_ref[pl.ds(side * half, half), :]
    part = got_ref[width:, :]
    kv = own_ref[0] + jnp.where(side == 0, part, whole)
    back = own_ref[1] + jnp.where(side == 0, whole, part)
    pairs = count // 2
    for z in range(2):
        cut = slice(z * rows, (z + 1) * rows)
        for x in range(pairs):
            takes_kv = jnp.logical_or(x > me // 2, (x == me // 2) & (me % 2 == 0))
            out_ref[z * pairs + x] = jnp.where(takes_kv, kv[cut], back[cut])


def gather_kernel(parts_ref, send_ref):
    pair = lax.axis_index("seq") // 2
    zero = jnp.zeros(parts_ref.shape[1:], F32)
    earlier, later = zero, zero
    pairs = parts_ref.shape[0] // 2
    for x in range(pairs):
        y = pairs - 1 - x
        for z in range(2):
            earlier = earlier + jnp.where(x < pair, parts_ref[z * pairs + x], zero)
            later = later + jnp.where(y > pair, parts_ref[z * pairs + y], zero)
    with_first = earlier + parts_ref[pair]
    with_second = later + parts_ref[pairs + pair]
    for side in range(2):
        send_ref[2 * side, 0] = earlier
        send_ref[2 * side, 1] = with_second
        send_ref[2 * side + 1, 0] = with_first
        send_ref[2 * side + 1, 1] = later


def final_kernel(
    q_ref, k_ref, v_ref, g_ref, scale_ref, state_ref, got_ref, keep_ref, *refs
):
    local, outs = refs[:4], refs[4:8]
    buffers, here, sems = refs[8:12], refs[12:16], refs[16]
    half_rows, width = q_ref.shape
    is_second = lax.axis_index("inner") % 2 == 1
    kv0, back1 = (
        jnp.concatenate([state_ref[j, i] for j in range(4)], 0)
        for i in range(2)
    )
    other = got_ref[:width, :]
    kv0 = kv0 + jnp.where(is_second, other, 0.0)
    back1 = back1 + jnp.where(is_second, 0.0, other)
    kv_used = [kv0.astype(BF16), (kv0 + keep_ref[:width, :]).astype(BF16)]
    back_used = [(back1 + keep_ref[width:, :]).astype(BF16), back1.astype(BF16)]

    def finish(local):
        copies = []

        def put(i, value, rows):
            buffers[i][rows, :] = value.astype(BF16)
            copy = pltpu.make_async_copy(
                buffers[i].at[rows, :], outs[i].at[rows, :], sems.at[len(copies)]
            )
            copy.start()
            copies.append(copy)

        for b in range(half_rows // BLOCK):
            rows = pl.ds(b * BLOCK, BLOCK)
            q, k, v, g = q_ref[rows, :], k_ref[rows, :], v_ref[rows, :], g_ref[rows, :]
            att, qg, kg, vg = (ref[rows, :] for ref in local)
            put(1, qg + dot(g, kv_used[b], 1, 1), rows)
            put(2, kg + dot(v, back_used[b], 1, 1), rows)
            put(3, vg + dot(k, back_used[b], 1, 0), rows)
            put(0, (att + dot(q, kv_used[b], 1, 0)) * scale_ref[rows, :], rows)
        for copy in copies:
            copy.wait()

    ready = waits_at_start()

    @pl.when(ready)
    def _():
        finish(local)

    @pl.when(jnp.logical_not(ready))
    def _():
        in_block(q_ref, k_ref, v_ref, g_ref, here)
        finish(here)


def in_memory(array):
    return pltpu.with_memory_space_constraint(array, pltpu.HBM)


def call(kernel, outs, limit, **options):
    return pl.pallas_call(
        kernel,
        out_shape=outs,
        compiler_params=pltpu.CompilerParams(vmem_limit_bytes=limit),
        **options,
    )


def per_device(pairs, lines, groups, queries, key_vectors, value_vectors, out_grad):
    half_rows, width = queries.shape
    blocks = half_rows // BLOCK
    rows16 = jax.ShapeDtypeStruct((half_rows, width), BF16)
    rows32 = jax.ShapeDtypeStruct((half_rows, width), F32)
    states = jax.ShapeDtypeStruct((2 * width, width), F32)
    half = width // 2
    halves = jax.ShapeDtypeStruct((2, half, width), F32)
    sent = jax.ShapeDtypeStruct((width + half, width), F32)
    in_hbm = pl.BlockSpec(memory_space=pltpu.HBM)
    send, own, keep, q, k, v, grad, scale, *local = call(
        outer_kernel,
        (sent, halves, states) + (rows16,) * 4 + (rows32,) * 5,
        2**24,
        in_specs=[in_hbm] * 4,
        scratch_shapes=[
            pltpu.VMEM((half_rows, width), BF16),
            pltpu.VMEM((2, width, width), F32),
            pltpu.SemaphoreType.DMA((4,)),
        ],
    )(*(in_memory(x) for x in (queries, key_vectors, value_vectors, out_grad)))

    got = lax.ppermute(send, AXES, pairs)
    count = lax.axis_size("seq")
    quarter = half // 2
    parts = call(
        spread_kernel,
        jax.ShapeDtypeStruct((count, quarter, width), F32),
        2**23,
    )(own, got)
    parts = lax.all_to_all(parts, AXES, 0, 0, axis_index_groups=lines)
    quads = jax.ShapeDtypeStruct((4, 2, quarter, width), F32)
    state = call(gather_kernel, quads, 2**23)(parts)
    state = lax.all_to_all(state, AXES, 0, 0, axis_index_groups=groups)
    return call(
        final_kernel,
        (rows16,) * 4,
        2**24,
        out_specs=(in_hbm,) * 4,
        scratch_shapes=[pltpu.VMEM((half_rows, width), BF16)] * 4
        + [pltpu.VMEM((half_rows, width), F32)] * 4
        + [pltpu.SemaphoreType.DMA((4 * blocks,))],
    )(q, k, v, grad, scale, state, got, keep, *local)


def solution(mesh):
    n_seq, n_inner = mesh.shape["seq"], mesh.shape["inner"]
    pairs = [(i, i ^ 1) for i in range(n_seq * n_inner)]
    lines = [
        [(2 * x + z) * n_inner + i for z in range(2) for x in range(n_seq // 2)]
        for i in range(n_inner)
    ]
    groups = [
        [(2 * x + z) * n_inner + 2 * h + side for side in range(2) for z in range(2)]
        for x in range(n_seq // 2)
        for h in range(n_inner // 2)
    ]
    spec = P("seq", "inner")
    return jax.shard_map(
        functools.partial(per_device, pairs, lines, groups),
        mesh=mesh,
        in_specs=(spec,) * 4,
        out_specs=(spec,) * 4,
        check_vma=False,
    )
```

```python
import functools

import jax
import jax.numpy as jnp
from jax import lax
from jax.experimental import pallas as pl
from jax.experimental.pallas import tpu as pltpu
from jax.sharding import PartitionSpec as P

BLOCK = 512
SUB = 256
AXES = ("seq", "inner")
F32 = jnp.float32
BF16 = jnp.bfloat16


def dot(a, b, ca, cb):
    return lax.dot_general(a, b, (((ca,), (cb,)), ((), ())), preferred_element_type=F32)


def scaling_of(start, rows, width):
    row = lax.broadcasted_iota(jnp.int32, (rows, width), 0)
    position = (start + row).astype(F32)
    return lax.rsqrt(width * (position + 1.0))


def first_position(half_rows):
    return (lax.axis_index("seq") * 2 + lax.axis_index("inner") % 2) * half_rows


def waits_at_start():
    place = lax.axis_index("inner")
    near = (place > 0) & (place < lax.axis_size("inner") // 4)
    return (lax.axis_index("seq") == 0) & near


def in_block(q_ref, k_ref, v_ref, g_ref, outs):
    att_ref, qg_ref, kg_ref, vg_ref = outs
    row = lax.broadcasted_iota(jnp.int32, (SUB, SUB), 0)
    col = lax.broadcasted_iota(jnp.int32, (SUB, SUB), 1)
    causal = row >= col
    n = BLOCK // SUB
    blocks = range(q_ref.shape[0] // BLOCK)

    def tiles(b, first, count):
        return pl.ds(b * BLOCK + first * SUB, count * SUB)

    def masked(scores):
        left = scores.shape[1] - SUB
        last = jnp.where(causal, scores[:, left:], 0.0)
        if left:
            last = jnp.concatenate([scores[:, :left], last], 1)
        return last.astype(BF16)

    weights, scores = {}, {}
    for b in blocks:
        for i in range(n):
            own, before = tiles(b, i, 1), tiles(b, 0, i + 1)
            weights[b, i] = masked(dot(q_ref[own, :], k_ref[before, :], 1, 1))
            scores[b, i] = masked(dot(g_ref[own, :], v_ref[before, :], 1, 1))
    for b in blocks:
        for i in range(n):
            own, before = tiles(b, i, 1), tiles(b, 0, i + 1)
            att_ref[own, :] = dot(weights[b, i], v_ref[before, :], 1, 0)
            qg_ref[own, :] = dot(scores[b, i], k_ref[before, :], 1, 0)
    for b in blocks:
        for j in range(n):
            own, after = tiles(b, j, 1), tiles(b, j, n - j)
            cut = slice(j * SUB, (j + 1) * SUB)
            w = jnp.concatenate([weights[b, i][:, cut] for i in range(j, n)], 0)
            s = jnp.concatenate([scores[b, i][:, cut] for i in range(j, n)], 0)
            vg_ref[own, :] = dot(w, g_ref[after, :], 0, 0)
            kg_ref[own, :] = dot(s, q_ref[after, :], 0, 0)


def outer_kernel(
    q_hbm, k_hbm, v_hbm, o_hbm,
    send_ref, own_ref, keep_ref, q_ref, k_ref, v_ref, grad_ref, scale_ref,
    att_ref, qg_ref, kg_ref, vg_ref,
    o_ref, total_ref, sems,
):
    half_rows, width = q_ref.shape
    start = first_position(half_rows)
    pairs = ((k_hbm, k_ref), (v_hbm, v_ref), (o_hbm, o_ref), (q_hbm, q_ref))
    copies = [
        pltpu.make_async_copy(source, target, sems.at[i])
        for i, (source, target) in enumerate(pairs)
    ]
    for copy in copies:
        copy.start()
    scale_ref[...] = scaling_of(start, half_rows, width)
    for copy in copies:
        copy.wait()
    kv, back = [], []
    for b in range(half_rows // BLOCK):
        rows = pl.ds(b * BLOCK, BLOCK)
        grad = (scale_ref[rows, :] * o_ref[rows, :].astype(F32)).astype(BF16)
        grad_ref[rows, :] = grad
        kv.append(dot(k_ref[rows, :], v_ref[rows, :], 0, 0))
        back.append(dot(q_ref[rows, :], grad, 0, 0))
    keep_ref[:width, :] = kv[0]
    keep_ref[width:, :] = back[1]
    half = width // 2
    side = lax.axis_index("inner") % 2
    total_ref[0] = kv[0] + kv[1]
    total_ref[1] = back[0] + back[1]
    own_ref[0] = total_ref[0, pl.ds(side * half, half), :]
    own_ref[1] = total_ref[1, pl.ds(side * half, half), :]
    send_ref[:width, :] = total_ref[side]
    send_ref[width:, :] = total_ref[1 - side, pl.ds((1 - side) * half, half), :]

    @pl.when(waits_at_start())
    def _():
        in_block(q_ref, k_ref, v_ref, grad_ref, (att_ref, qg_ref, kg_ref, vg_ref))


def spread_kernel(own_ref, got_ref, out_ref):
    count, rows, width = out_ref.shape
    half = width // 2
    me = lax.axis_index("seq")
    side = lax.axis_index("inner") % 2
    whole = got_ref[pl.ds(side * half, half), :]
    part = got_ref[width:, :]
    kv = own_ref[0] + jnp.where(side == 0, part, whole)
    back = own_ref[1] + jnp.where(side == 0, whole, part)
    pairs = count // 2
    for z in range(2):
        cut = slice(z * rows, (z + 1) * rows)
        for x in range(pairs):
            takes_kv = jnp.logical_or(x > me // 2, (x == me // 2) & (me % 2 == 0))
            out_ref[z * pairs + pairs - 1 - x] = jnp.where(takes_kv, kv[cut], back[cut])


def gather_kernel(parts_ref, send_ref):
    pair = lax.axis_index("seq") // 2
    zero = jnp.zeros(parts_ref.shape[1:], F32)
    earlier, later = zero, zero
    pairs = parts_ref.shape[0] // 2
    for x in range(pairs):
        y = pairs - 1 - x
        for z in range(2):
            earlier = earlier + jnp.where(x < pair, parts_ref[z * pairs + y], zero)
            later = later + jnp.where(y > pair, parts_ref[z * pairs + x], zero)
    with_first = earlier + parts_ref[pairs - 1 - pair]
    with_second = later + parts_ref[2 * pairs - 1 - pair]
    for side in range(2):
        send_ref[2 * side, 0] = earlier
        send_ref[2 * side, 1] = with_second
        send_ref[2 * side + 1, 0] = with_first
        send_ref[2 * side + 1, 1] = later


def final_kernel(
    q_ref, k_ref, v_ref, g_ref, scale_ref, state_ref, got_ref, keep_ref, *refs
):
    local, outs = refs[:4], refs[4:8]
    buffers, here, sems = refs[8:12], refs[12:16], refs[16]
    half_rows, width = q_ref.shape
    is_second = lax.axis_index("inner") % 2 == 1
    kv0, back1 = (
        jnp.concatenate([state_ref[j, i] for j in range(4)], 0)
        for i in range(2)
    )
    other = got_ref[:width, :]
    kv0 = kv0 + jnp.where(is_second, other, 0.0)
    back1 = back1 + jnp.where(is_second, 0.0, other)
    kv_used = [kv0.astype(BF16), (kv0 + keep_ref[:width, :]).astype(BF16)]
    back_used = [(back1 + keep_ref[width:, :]).astype(BF16), back1.astype(BF16)]

    def finish(local):
        copies = []

        def put(i, value, rows):
            buffers[i][rows, :] = value.astype(BF16)
            copy = pltpu.make_async_copy(
                buffers[i].at[rows, :], outs[i].at[rows, :], sems.at[len(copies)]
            )
            copy.start()
            copies.append(copy)

        for b in range(half_rows // BLOCK):
            rows = pl.ds(b * BLOCK, BLOCK)
            q, k, v, g = q_ref[rows, :], k_ref[rows, :], v_ref[rows, :], g_ref[rows, :]
            att, qg, kg, vg = (ref[rows, :] for ref in local)
            put(1, qg + dot(g, kv_used[b], 1, 1), rows)
            put(2, kg + dot(v, back_used[b], 1, 1), rows)
            put(3, vg + dot(k, back_used[b], 1, 0), rows)
            put(0, (att + dot(q, kv_used[b], 1, 0)) * scale_ref[rows, :], rows)
        for copy in copies:
            copy.wait()

    ready = waits_at_start()

    @pl.when(ready)
    def _():
        finish(local)

    @pl.when(jnp.logical_not(ready))
    def _():
        in_block(q_ref, k_ref, v_ref, g_ref, here)
        finish(here)


def in_memory(array):
    return pltpu.with_memory_space_constraint(array, pltpu.HBM)


def call(kernel, outs, limit, **options):
    return pl.pallas_call(
        kernel,
        out_shape=outs,
        compiler_params=pltpu.CompilerParams(vmem_limit_bytes=limit),
        **options,
    )


def per_device(pairs, lines, groups, queries, key_vectors, value_vectors, out_grad):
    half_rows, width = queries.shape
    blocks = half_rows // BLOCK
    rows16 = jax.ShapeDtypeStruct((half_rows, width), BF16)
    rows32 = jax.ShapeDtypeStruct((half_rows, width), F32)
    states = jax.ShapeDtypeStruct((2 * width, width), F32)
    half = width // 2
    halves = jax.ShapeDtypeStruct((2, half, width), F32)
    sent = jax.ShapeDtypeStruct((width + half, width), F32)
    in_hbm = pl.BlockSpec(memory_space=pltpu.HBM)
    send, own, keep, q, k, v, grad, scale, *local = call(
        outer_kernel,
        (sent, halves, states) + (rows16,) * 4 + (rows32,) * 5,
        2**24,
        in_specs=[in_hbm] * 4,
        scratch_shapes=[
            pltpu.VMEM((half_rows, width), BF16),
            pltpu.VMEM((2, width, width), F32),
            pltpu.SemaphoreType.DMA((4,)),
        ],
    )(*(in_memory(x) for x in (queries, key_vectors, value_vectors, out_grad)))

    got = lax.ppermute(send, AXES, pairs)
    count = lax.axis_size("seq")
    quarter = half // 2
    parts = call(
        spread_kernel,
        jax.ShapeDtypeStruct((count, quarter, width), F32),
        2**23,
    )(own, got)
    parts = lax.all_to_all(parts, AXES, 0, 0, axis_index_groups=lines)
    quads = jax.ShapeDtypeStruct((4, 2, quarter, width), F32)
    state = call(gather_kernel, quads, 2**23)(parts)
    state = lax.all_to_all(state, AXES, 0, 0, axis_index_groups=groups)
    return call(
        final_kernel,
        (rows16,) * 4,
        2**24,
        out_specs=(in_hbm,) * 4,
        scratch_shapes=[pltpu.VMEM((half_rows, width), BF16)] * 4
        + [pltpu.VMEM((half_rows, width), F32)] * 4
        + [pltpu.SemaphoreType.DMA((4 * blocks,))],
    )(q, k, v, grad, scale, state, got, keep, *local)


def solution(mesh):
    n_seq, n_inner = mesh.shape["seq"], mesh.shape["inner"]
    pairs = [(i, i ^ 1) for i in range(n_seq * n_inner)]
    lines = [
        [(2 * x + z) * n_inner + i for z in range(2) for x in reversed(range(n_seq // 2))]
        for i in range(n_inner)
    ]
    groups = [
        [(2 * x + z) * n_inner + 2 * h + side for side in range(2) for z in range(2)]
        for x in range(n_seq // 2)
        for h in range(n_inner // 2)
    ]
    spec = P("seq", "inner")
    return jax.shard_map(
        functools.partial(per_device, pairs, lines, groups),
        mesh=mesh,
        in_specs=(spec,) * 4,
        out_specs=(spec,) * 4,
        check_vma=False,
    )
```
